32 devices in a mesh: groups: 2 (over x), blk: 8 (over z, y), sub: 2 (over core).
Axes of the slice: x: 2, y: 2, z: 4, core: 2. Of those that a mesh axis runs over, the one named last changes fastest.
Arguments:
- queries: bfloat16 [2048, 4096], P(('groups', 'blk'), 'sub'), parts along dimension 0, may hold values from -6 to 6
- passages: bfloat16 [2048, 4096], P(('groups', 'blk'), 'sub'), parts along dimension 0, may hold values from -6 to 6
- negatives: int32 [2048, 7], P(('groups', 'blk')), parts along dimension 0, may hold values from 0 to 1023, as said below
Outputs:
- grad_queries: bfloat16 [2048, 4096], P(('groups', 'blk'), 'sub'), parts along dimension 0
- grad_passages: bfloat16 [2048, 4096], P(('groups', 'blk'), 'sub'), parts along dimension 0
The draws below stay inside these ranges and needn't reach their ends.
There are 2 independent parts, one for each index of `groups`. The reference program is written for one: setup_inputs(seed, part) draws one part's arguments, and reference() takes and returns one part's arrays. A program takes and returns all parts, laid end to end along the dimension named above; each array names one. Nothing has to cross between parts.
Inputs may be any that keep to these rules, and one draw needn't show every extreme that they name: `negatives`: passage j lies in block j // 128. Among the 896 entries of one block of queries (rows of one device along blk), at most 128 name passages of any one block; in every draw some blocks are named exactly 128 times by the entries of every block of queries.
All inputs are finite; a program needn't handle non-finite values.
Results may differ from the reference program's by a relative error of at most 0.005.
Values may be sent and summed in bfloat16 or wider, within the bound.
A program may use at most 64 MiB of HBM per device.

```python
import math
import jax
import jax.numpy as jnp
from jax import lax

D = 4096
ROWS = 128
NEG = 7
HALF = 2
QUERIES = 1024
PASSAGES = 1024


def draw_negatives(key, part):
    key = jax.random.fold_in(key, 11)
    owners = PASSAGES // ROWS
    hot_count = owners // 8
    capacity = 8 * ROWS // owners
    slot_count = NEG * ROWS
    seat_count = owners * capacity
    key_hot, key_seat, key_first, key_second = jax.random.split(key, 4)
    ranking = jax.random.permutation(key_hot, owners)
    hot_owner = ranking < hot_count
    seat_owner = jnp.arange(seat_count, dtype=jnp.int32) // capacity
    seat_hot = hot_owner[seat_owner]

    def one_source(source_key):
        order_key, shuffle_key = jax.random.split(source_key)
        order = jax.random.permutation(order_key, seat_count).astype(jnp.int32)
        priority = order + jnp.where(seat_hot, 0, seat_count).astype(jnp.int32)
        chosen = jnp.argsort(priority, stable=True)[:slot_count]
        owner_of = seat_owner[chosen]
        return owner_of[jax.random.permutation(shuffle_key, slot_count)]
    owner_table = jax.vmap(one_source)(jax.random.split(key_seat, owners))
    first_pick = jax.random.randint(key_first, (owners, slot_count), 0, ROWS, dtype=jnp.int32)
    second_pick = jax.random.randint(key_second, (owners, slot_count), 0, ROWS, dtype=jnp.int32)
    local_row = first_pick * second_pick // ROWS
    result = owner_table.astype(jnp.int32) * ROWS + local_row
    return result.reshape(owners * ROWS, NEG).astype(jnp.int32)


def level_of(key, shape, shards, least, largest):
    loudness, own = 1.0, jax.random.fold_in(key, 6)
    for axis_at, parts in shards:
        heights = jnp.exp(jax.random.uniform(jax.random.fold_in(own, axis_at), (parts,), jnp.float32, least / len(shards), largest / len(shards)))
        loudness = loudness * jnp.repeat(heights, shape[axis_at] // parts).reshape([-1 if axis == axis_at else 1 for axis in range(len(shape))])
    return loudness


def bell_draw(rng, extent, deviation, bound, pieces=(), kind=jnp.bfloat16):
    level = level_of(rng, extent, pieces, -0.22, 0.18) if pieces else 1.0
    values = jax.random.normal(rng, extent, jnp.float32) * deviation * level
    return jnp.minimum(jnp.maximum(values, -bound), bound).astype(kind)


def setup_inputs(seed: int = 0, part: int = 0) -> dict:
    key_list = jax.random.split(jax.random.key(seed), 4)
    own_keys = jax.random.split(jax.random.fold_in(key_list[3], part), 4)
    return {
        "queries": bell_draw(own_keys[0], (QUERIES, D), 1.0, 6.0, ((0, 8), (1, 2))),
        "passages": bell_draw(own_keys[1], (PASSAGES, D), 1.0, 6.0, ((0, 8), (1, 2))),
        "negatives": draw_negatives(jax.random.fold_in(jax.random.fold_in(key_list[3], part), 71), part),
    }


LOGIT_SLOPE = 2.0
LOGIT_SHIFT = -1.0
HARD_WEIGHT = 2.0

def reference(queries, passages, negatives):
    factor = LOGIT_SLOPE / math.sqrt(D)
    blocks = QUERIES // ROWS
    query_blocks = queries.reshape(blocks, ROWS, D)
    passage_blocks = passages.reshape(blocks, ROWS, D)
    neg_blocks = negatives.reshape(blocks, ROWS, NEG)
    identity_tile = jnp.eye(ROWS, dtype=jnp.float32)

    def query_side(block_index):
        query_rows = query_blocks[block_index]
        summed = jnp.zeros((ROWS, D), jnp.float32)
        tiles = []
        for offset in range(-HALF, HALF + 1):
            passage_rows = passage_blocks[(block_index + offset) % blocks]
            logits = factor * jnp.dot(query_rows, passage_rows.T, preferred_element_type=jnp.float32) + LOGIT_SHIFT
            weights = jax.nn.sigmoid(logits)
            if offset == 0:
                weights = weights - identity_tile
            coeffs = weights.astype(jnp.bfloat16)
            tiles.append(coeffs)
            summed = summed + jnp.dot(coeffs, passage_rows, preferred_element_type=jnp.float32)
        hard_rows = passages[neg_blocks[block_index]]
        hard_scores = jnp.einsum('rkd,rd->rk', hard_rows.astype(jnp.float32), query_rows.astype(jnp.float32), precision=lax.Precision.HIGHEST)
        hard_coeffs = (HARD_WEIGHT * jax.nn.sigmoid(factor * hard_scores + LOGIT_SHIFT)).astype(jnp.bfloat16)
        summed = summed + jnp.einsum('rk,rkd->rd', hard_coeffs.astype(jnp.float32), hard_rows.astype(jnp.float32), precision=lax.Precision.HIGHEST)
        return (summed, jnp.stack(tiles), hard_coeffs)
    block_ids = jnp.arange(blocks, dtype=jnp.int32)
    query_sums, tile_table, hard_table = lax.map(query_side, block_ids)

    def passage_side(block_index):
        summed = jnp.zeros((ROWS, D), jnp.float32)
        for turn_index, offset in enumerate(range(-HALF, HALF + 1)):
            source = (block_index - offset) % blocks
            coeffs = tile_table[source, turn_index]
            summed = summed + jnp.dot(coeffs.T, query_blocks[source], preferred_element_type=jnp.float32)
        return summed
    window_sums = lax.map(passage_side, block_ids)

    def add_hard(carry, block_index):
        terms = hard_table[block_index].astype(jnp.float32)[:, :, None] * query_blocks[block_index].astype(jnp.float32)[:, None, :]
        carry = carry.at[neg_blocks[block_index].reshape(-1)].add(terms.reshape(ROWS * NEG, D))
        return (carry, None)
    hard_sums, _ = lax.scan(add_hard, jnp.zeros((PASSAGES, D), jnp.float32), block_ids)
    grad_queries = (factor * query_sums.reshape(QUERIES, D)).astype(jnp.bfloat16)
    grad_passages = (factor * (window_sums.reshape(PASSAGES, D) + hard_sums)).astype(jnp.bfloat16)
    return (grad_queries, grad_passages)
```

```python
import math

import jax
import jax.numpy as jnp
from jax import lax
from jax.sharding import PartitionSpec as P

D = 4096
HALF = 2


LOGIT_SLOPE = 2.0
LOGIT_SHIFT = -1.0
HARD_WEIGHT = 2.0


def shifted(value, axis, steps):
    count = lax.axis_size(axis)
    pairs = [(source, (source + steps) % count) for source in range(count)]
    return lax.ppermute(value, axis, pairs)


def tile_step(queries, passage_rows, carried, grad_rows, offset, factor):
    partial_value = jnp.einsum(
        "id,jd->ij", queries, passage_rows, preferred_element_type=jnp.float32
    )
    scores = lax.psum(partial_value, "sub")
    weights = jax.nn.sigmoid(factor * scores + LOGIT_SHIFT)
    if offset == 0:
        weights = weights - jnp.eye(weights.shape[0], dtype=jnp.float32)
    coeffs = weights.astype(jnp.bfloat16)
    grad_rows = grad_rows + jnp.dot(coeffs, passage_rows, preferred_element_type=jnp.float32)
    carried = carried + jnp.einsum("ij,id->jd", coeffs, queries, preferred_element_type=jnp.float32)
    return (carried, grad_rows)


def local(queries, passages, negatives):
    factor = LOGIT_SLOPE / math.sqrt(D)
    row_count, width = queries.shape
    zeros_tile = jnp.zeros((row_count, width), jnp.float32)
    grad_rows = zeros_tile
    upper_block = passages
    lower_block = shifted(passages, "blk", 1)
    upper_accum = zeros_tile
    lower_accum = zeros_tile
    for turn_index in range(HALF + 1):
        upper_accum, grad_rows = tile_step(
            queries, upper_block, upper_accum, grad_rows, turn_index, factor
        )
        if turn_index < HALF:
            lower_accum, grad_rows = tile_step(
                queries, lower_block, lower_accum, grad_rows, -(turn_index + 1), factor
            )
            upper_block = shifted(upper_block, "blk", -1)
            upper_accum = shifted(upper_accum, "blk", -1)
        if turn_index < HALF - 1:
            lower_block = shifted(lower_block, "blk", 1)
            lower_accum = shifted(lower_accum.astype(jnp.bfloat16), "blk", 1).astype(
                lower_accum.dtype
            )
    window_pass = shifted(upper_accum, "blk", HALF) + shifted(lower_accum, "blk", -HALF)
    owners = lax.axis_size("blk")
    neg_count = negatives.shape[1]
    capacity = 8 * row_count // owners
    slot_count = row_count * neg_count
    flat_neg = negatives.reshape(-1)
    owner_of = flat_neg // row_count
    local_row = flat_neg % row_count
    onehot_owner = (owner_of[:, None] == jnp.arange(owners, dtype=jnp.int32)[None, :]).astype(
        jnp.int32
    )
    position = jnp.sum((jnp.cumsum(onehot_owner, axis=0) - 1) * onehot_owner, axis=1)
    slot_index = owner_of * capacity + position
    requests = (
        jnp.full((owners * capacity,), -1, jnp.int32)
        .at[slot_index]
        .set(local_row)
        .reshape(owners, capacity)
    )
    incoming = lax.all_to_all(requests, "blk", split_axis=0, concat_axis=0, tiled=True)
    is_live = incoming >= 0
    picked = jnp.where(is_live, incoming, 0)
    rows_out = jnp.take(passages, picked.reshape(-1), axis=0).reshape(owners, capacity, width)
    fetched = lax.all_to_all(rows_out, "blk", split_axis=0, concat_axis=0, tiled=True)
    slot_rows = jnp.take(fetched.reshape(owners * capacity, width), slot_index, axis=0).reshape(
        row_count, neg_count, width
    )
    hard_partial = jnp.einsum("rkd,rd->rk", slot_rows, queries, preferred_element_type=jnp.float32)
    hard_scores = lax.psum(hard_partial, "sub")
    hard_coeffs = (HARD_WEIGHT * jax.nn.sigmoid(factor * hard_scores + LOGIT_SHIFT)).astype(
        jnp.bfloat16
    )
    grad_rows = grad_rows + jnp.einsum(
        "rk,rkd->rd", hard_coeffs, slot_rows, preferred_element_type=jnp.float32
    )
    source_slot = (
        jnp.zeros((owners * capacity,), jnp.int32)
        .at[slot_index]
        .set(jnp.arange(slot_count, dtype=jnp.int32))
    )
    query_buffer = jnp.take(queries, source_slot // neg_count, axis=0).reshape(
        owners, capacity, width
    )
    arrived_rows = lax.all_to_all(query_buffer, "blk", split_axis=0, concat_axis=0, tiled=True)
    owner_partial = jnp.einsum(
        "scd,scd->sc", arrived_rows, rows_out, preferred_element_type=jnp.float32
    )
    owner_scores = lax.psum(owner_partial, "sub")
    owner_coeffs = jnp.where(
        is_live, HARD_WEIGHT * jax.nn.sigmoid(factor * owner_scores + LOGIT_SHIFT), 0.0
    ).astype(jnp.bfloat16)
    member = (
        jnp.arange(row_count, dtype=jnp.int32)[:, None] == picked.reshape(1, -1)
    ) & is_live.reshape(1, -1)
    weighted = jnp.where(member, owner_coeffs.reshape(1, -1), jnp.zeros((), jnp.bfloat16))
    hard_pass = jnp.dot(
        weighted, arrived_rows.reshape(owners * capacity, width), preferred_element_type=jnp.float32
    )
    grad_queries = (factor * grad_rows).astype(jnp.bfloat16)
    grad_passages = (factor * (window_pass + hard_pass)).astype(jnp.bfloat16)
    return (grad_queries, grad_passages)


def pair_weights(scores, counts, near, diagonal, factor):
    gate = jax.nn.sigmoid(factor * scores + LOGIT_SHIFT)
    window = jnp.where(near, gate - diagonal, 0.0).astype(jnp.bfloat16).astype(jnp.float32)
    hard = (HARD_WEIGHT * gate).astype(jnp.bfloat16).astype(jnp.float32)
    return (window + counts * hard).astype(jnp.bfloat16)


def dense_local(queries, passages, negatives):
    factor = LOGIT_SLOPE / math.sqrt(D)
    row_count, width = queries.shape
    owners = lax.axis_size("blk")
    me = lax.axis_index("blk")
    total = owners * row_count
    all_passages = lax.all_gather(passages, "blk", axis=0, tiled=True)
    all_queries = lax.all_gather(queries, "blk", axis=0, tiled=True)
    all_negatives = lax.all_gather(negatives, "blk", axis=0, tiled=True)
    row_part = jnp.einsum("id,jd->ij", queries, all_passages, preferred_element_type=jnp.float32)
    col_part = jnp.einsum("jd,id->ji", passages, all_queries, preferred_element_type=jnp.float32)
    row_scores, col_scores = lax.psum((row_part, col_part), "sub")
    mine = me * row_count + lax.broadcasted_iota(jnp.int32, (row_count, total), 0)
    other = lax.broadcasted_iota(jnp.int32, (row_count, total), 1)
    gap = (other // row_count - me + HALF + owners) % owners
    near = gap <= 2 * HALF
    diagonal = (mine == other).astype(jnp.float32)
    row_counts = jnp.zeros((row_count, total), jnp.float32)
    col_counts = jnp.zeros((row_count, total), jnp.float32)
    turned = all_negatives.T
    for k in range(negatives.shape[1]):
        row_counts += (negatives[:, k : k + 1] == other).astype(jnp.float32)
        col_counts += (turned[k : k + 1, :] == mine).astype(jnp.float32)
    row_w = pair_weights(row_scores, row_counts, near, diagonal, factor)
    col_w = pair_weights(col_scores, col_counts, near, diagonal, factor)
    grad_queries = factor * jnp.dot(row_w, all_passages, preferred_element_type=jnp.float32)
    grad_passages = factor * jnp.dot(col_w, all_queries, preferred_element_type=jnp.float32)
    return (grad_queries.astype(jnp.bfloat16), grad_passages.astype(jnp.bfloat16))


def solution(mesh):
    owners = mesh.shape["blk"]
    body = dense_local if owners == 8 else local
    return jax.shard_map(
        body,
        mesh=mesh,
        in_specs=(
            P(("groups", "blk"), "sub"),
            P(("groups", "blk"), "sub"),
            P(("groups", "blk"), None),
        ),
        out_specs=(P(("groups", "blk"), "sub"), P(("groups", "blk"), "sub")),
        check_vma=False,
    )
```

```python
import functools
import math

import jax
import jax.numpy as jnp
from jax import lax
from jax.experimental import pallas as pl
from jax.experimental.pallas import tpu as pltpu
from jax.sharding import PartitionSpec as P

D = 4096
HALF = 2


LOGIT_SLOPE = 2.0
LOGIT_SHIFT = -1.0
HARD_WEIGHT = 2.0


def shifted(value, axis, steps):
    count = lax.axis_size(axis)
    pairs = [(source, (source + steps) % count) for source in range(count)]
    return lax.ppermute(value, axis, pairs)


def tile_step(queries, passage_rows, carried, grad_rows, offset, factor):
    partial_value = jnp.einsum(
        "id,jd->ij", queries, passage_rows, preferred_element_type=jnp.float32
    )
    scores = lax.psum(partial_value, "sub")
    weights = jax.nn.sigmoid(factor * scores + LOGIT_SHIFT)
    if offset == 0:
        weights = weights - jnp.eye(weights.shape[0], dtype=jnp.float32)
    coeffs = weights.astype(jnp.bfloat16)
    grad_rows = grad_rows + jnp.dot(coeffs, passage_rows, preferred_element_type=jnp.float32)
    carried = carried + jnp.einsum("ij,id->jd", coeffs, queries, preferred_element_type=jnp.float32)
    return (carried, grad_rows)


def local(queries, passages, negatives):
    factor = LOGIT_SLOPE / math.sqrt(D)
    row_count, width = queries.shape
    zeros_tile = jnp.zeros((row_count, width), jnp.float32)
    grad_rows = zeros_tile
    upper_block = passages
    lower_block = shifted(passages, "blk", 1)
    upper_accum = zeros_tile
    lower_accum = zeros_tile
    for turn_index in range(HALF + 1):
        upper_accum, grad_rows = tile_step(
            queries, upper_block, upper_accum, grad_rows, turn_index, factor
        )
        if turn_index < HALF:
            lower_accum, grad_rows = tile_step(
                queries, lower_block, lower_accum, grad_rows, -(turn_index + 1), factor
            )
            upper_block = shifted(upper_block, "blk", -1)
            upper_accum = shifted(upper_accum, "blk", -1)
        if turn_index < HALF - 1:
            lower_block = shifted(lower_block, "blk", 1)
            lower_accum = shifted(lower_accum.astype(jnp.bfloat16), "blk", 1).astype(
                lower_accum.dtype
            )
    window_pass = shifted(upper_accum, "blk", HALF) + shifted(lower_accum, "blk", -HALF)
    owners = lax.axis_size("blk")
    neg_count = negatives.shape[1]
    capacity = 8 * row_count // owners
    slot_count = row_count * neg_count
    flat_neg = negatives.reshape(-1)
    owner_of = flat_neg // row_count
    local_row = flat_neg % row_count
    onehot_owner = (owner_of[:, None] == jnp.arange(owners, dtype=jnp.int32)[None, :]).astype(
        jnp.int32
    )
    position = jnp.sum((jnp.cumsum(onehot_owner, axis=0) - 1) * onehot_owner, axis=1)
    slot_index = owner_of * capacity + position
    requests = (
        jnp.full((owners * capacity,), -1, jnp.int32)
        .at[slot_index]
        .set(local_row)
        .reshape(owners, capacity)
    )
    incoming = lax.all_to_all(requests, "blk", split_axis=0, concat_axis=0, tiled=True)
    is_live = incoming >= 0
    picked = jnp.where(is_live, incoming, 0)
    rows_out = jnp.take(passages, picked.reshape(-1), axis=0).reshape(owners, capacity, width)
    fetched = lax.all_to_all(rows_out, "blk", split_axis=0, concat_axis=0, tiled=True)
    slot_rows = jnp.take(fetched.reshape(owners * capacity, width), slot_index, axis=0).reshape(
        row_count, neg_count, width
    )
    hard_partial = jnp.einsum("rkd,rd->rk", slot_rows, queries, preferred_element_type=jnp.float32)
    hard_scores = lax.psum(hard_partial, "sub")
    hard_coeffs = (HARD_WEIGHT * jax.nn.sigmoid(factor * hard_scores + LOGIT_SHIFT)).astype(
        jnp.bfloat16
    )
    grad_rows = grad_rows + jnp.einsum(
        "rk,rkd->rd", hard_coeffs, slot_rows, preferred_element_type=jnp.float32
    )
    source_slot = (
        jnp.zeros((owners * capacity,), jnp.int32)
        .at[slot_index]
        .set(jnp.arange(slot_count, dtype=jnp.int32))
    )
    query_buffer = jnp.take(queries, source_slot // neg_count, axis=0).reshape(
        owners, capacity, width
    )
    arrived_rows = lax.all_to_all(query_buffer, "blk", split_axis=0, concat_axis=0, tiled=True)
    owner_partial = jnp.einsum(
        "scd,scd->sc", arrived_rows, rows_out, preferred_element_type=jnp.float32
    )
    owner_scores = lax.psum(owner_partial, "sub")
    owner_coeffs = jnp.where(
        is_live, HARD_WEIGHT * jax.nn.sigmoid(factor * owner_scores + LOGIT_SHIFT), 0.0
    ).astype(jnp.bfloat16)
    member = (
        jnp.arange(row_count, dtype=jnp.int32)[:, None] == picked.reshape(1, -1)
    ) & is_live.reshape(1, -1)
    weighted = jnp.where(member, owner_coeffs.reshape(1, -1), jnp.zeros((), jnp.bfloat16))
    hard_pass = jnp.dot(
        weighted, arrived_rows.reshape(owners * capacity, width), preferred_element_type=jnp.float32
    )
    grad_queries = (factor * grad_rows).astype(jnp.bfloat16)
    grad_passages = (factor * (window_pass + hard_pass)).astype(jnp.bfloat16)
    return (grad_queries, grad_passages)


def pair_weights(scores, counts, near, diagonal, factor):
    gate = jax.nn.sigmoid(factor * scores + LOGIT_SHIFT)
    window = jnp.where(near, gate - diagonal, 0.0).astype(jnp.bfloat16).astype(jnp.float32)
    hard = (HARD_WEIGHT * gate).astype(jnp.bfloat16).astype(jnp.float32)
    return (window + counts * hard).astype(jnp.bfloat16)


CHUNKS = 8
EARLY = 7
TILE = 512


def line_kernel(
    owners, neg_count, q_hbm, p_hbm, neg_ref, turned_ref, gq_ref, gp_ref,
    held, turned_all, own_part, other_part, row_w, col_w,
    load_sem, neg_send, neg_recv, up_send, down_send, cross_send, recv_sem, score_sem,
):
    factor = LOGIT_SLOPE / math.sqrt(D)
    row_count = q_hbm.shape[0]
    width = q_hbm.shape[1]
    chunk_rows = 2 * row_count // CHUNKS
    half = CHUNKS // 2
    line = owners // 2
    me = lax.axis_index("blk")
    side = lax.axis_index("sub")
    place = me // 2
    lane = me % 2
    partner = place * 2 + 1 - lane

    def chunk(block, piece):
        start = pl.multiple_of(block * row_count + (piece % half) * chunk_rows, chunk_rows)
        return held.at[piece // half, pl.ds(start, chunk_rows), :]

    def send(block, piece, sems, target):
        return pltpu.make_async_remote_copy(
            src_ref=chunk(block, piece), dst_ref=chunk(block, piece),
            send_sem=sems.at[block, piece], recv_sem=recv_sem.at[block, piece],
            device_id={"blk": target}, device_id_type=pl.DeviceIdType.MESH,
        )

    def upward(block, piece):
        return send(block, piece, up_send, me + 2)

    def downward(block, piece):
        return send(block, piece, down_send, me - 2)

    def across(block, piece):
        return send(block, piece, cross_send, partner)

    def arrived(block, piece):
        send(block, piece, cross_send, partner).wait_recv()

    own_rows = pl.ds(pl.multiple_of(me * row_count, row_count), row_count)
    loads = [
        pltpu.make_async_copy(q_hbm, held.at[0, own_rows, :], load_sem.at[0]),
        pltpu.make_async_copy(p_hbm, held.at[1, own_rows, :], load_sem.at[1]),
    ]
    for load in loads:
        load.start()
    barrier = pltpu.get_barrier_semaphore()
    for step in range(1, owners):
        pl.semaphore_signal(
            barrier, inc=1, device_id={"blk": (me + step) % owners},
            device_id_type=pl.DeviceIdType.MESH,
        )
    pl.semaphore_signal(
        barrier, inc=1, device_id={"sub": 1 - side}, device_id_type=pl.DeviceIdType.MESH
    )
    turned_all[me] = turned_ref[...]
    for load in loads:
        load.wait()
    pl.semaphore_wait(barrier, owners)

    @pl.loop(0, CHUNKS)
    def _(piece):
        @pl.when(place < line - 1)
        def _():
            upward(me, piece).start()

        @pl.when(place > 0)
        def _():
            downward(me, piece).start()

        across(me, piece).start()

    def neg_copy(step):
        return pltpu.make_async_remote_copy(
            src_ref=turned_all.at[me], dst_ref=turned_all.at[me],
            send_sem=neg_send.at[step], recv_sem=neg_recv.at[me],
            device_id={"blk": (me + step) % owners}, device_id_type=pl.DeviceIdType.MESH,
        )

    for step in range(1, owners):
        neg_copy(step).start()

    @pl.loop(EARLY, CHUNKS)
    def _(piece):
        arrived(partner, piece)

        @pl.when(place < line - 1)
        def _():
            upward(partner, piece).start()

        @pl.when(place > 0)
        def _():
            downward(partner, piece).start()

    for far in range(1, line):
        below = (place - far) * 2
        above = (place + far) * 2

        def forward(piece, row, cross):
            @pl.when(place >= far)
            def _():
                block = below + row
                arrived(block, piece)

                @pl.when(place < line - 1)
                def _():
                    upward(block, piece).start()

                if cross:
                    across(block, piece).start()

            @pl.when(place + far < line)
            def _():
                block = above + row
                arrived(block, piece)

                @pl.when(place > 0)
                def _():
                    downward(block, piece).start()

                if cross:
                    across(block, piece).start()

        @pl.loop(0, EARLY)
        def _(piece):
            forward(piece, lane, True)

        @pl.loop(EARLY, CHUNKS)
        def _(piece):
            forward(piece, lane, False)

        @pl.loop(EARLY, CHUNKS)
        def _(piece):
            forward(piece, 1 - lane, False)

    @pl.loop(0, line)
    def _(spot):
        @pl.loop(0, EARLY)
        def _(piece):
            arrived(spot * 2 + 1 - lane, piece)

    @pl.loop(0, owners)
    def _(block):
        rows = pl.ds(pl.multiple_of(block * row_count, row_count), row_count)
        own_part[0, block] = lax.dot_general(
            held[0, own_rows, :], held[1, rows, :], (((1,), (1,)), ((), ())),
            preferred_element_type=jnp.float32,
        )
        own_part[1, block] = lax.dot_general(
            held[1, own_rows, :], held[0, rows, :], (((1,), (1,)), ((), ())),
            preferred_element_type=jnp.float32,
        )

    swap = pltpu.make_async_remote_copy(
        src_ref=own_part, dst_ref=other_part, send_sem=score_sem.at[0], recv_sem=score_sem.at[1],
        device_id={"sub": 1 - side}, device_id_type=pl.DeviceIdType.MESH,
    )
    swap.start()
    for step in range(1, owners):
        block = (me + step) % owners
        pltpu.make_async_remote_copy(
            src_ref=turned_all.at[block], dst_ref=turned_all.at[block],
            send_sem=neg_send.at[step], recv_sem=neg_recv.at[block],
            device_id={"blk": block}, device_id_type=pl.DeviceIdType.MESH,
        ).wait_recv()
    swap.wait()

    down_index = lax.broadcasted_iota(jnp.int32, (row_count, row_count), 0)
    across_index = lax.broadcasted_iota(jnp.int32, (row_count, row_count), 1)

    @pl.loop(0, owners)
    def _(block):
        gap = (block - me + HALF + owners) % owners
        near = (jnp.zeros((row_count, row_count), jnp.int32) + gap) <= 2 * HALF
        diagonal = (down_index + me * row_count == across_index + block * row_count).astype(
            jnp.float32
        )
        row_counts = jnp.zeros((row_count, row_count), jnp.float32)
        col_counts = jnp.zeros((row_count, row_count), jnp.float32)
        for k in range(neg_count):
            row_counts += (
                neg_ref[:, k : k + 1] == across_index + block * row_count
            ).astype(jnp.float32)
            col_counts += (
                turned_all[block, k : k + 1, :] == down_index + me * row_count
            ).astype(jnp.float32)
        columns = pl.ds(pl.multiple_of(block * row_count, row_count), row_count)
        row_w[:, columns] = pair_weights(
            own_part[0, block] + other_part[0, block], row_counts, near, diagonal, factor
        )
        col_w[:, columns] = pair_weights(
            own_part[1, block] + other_part[1, block], col_counts, near, diagonal, factor
        )

    @pl.loop(0, width // TILE)
    def _(tile):
        columns = pl.ds(pl.multiple_of(tile * TILE, TILE), TILE)
        gq_ref[:, columns] = (
            factor
            * jnp.dot(row_w[...], held[1, :, columns], preferred_element_type=jnp.float32)
        ).astype(jnp.bfloat16)
        gp_ref[:, columns] = (
            factor
            * jnp.dot(col_w[...], held[0, :, columns], preferred_element_type=jnp.float32)
        ).astype(jnp.bfloat16)

    for step in range(1, owners):
        neg_copy(step).wait_send()

    def sent(block, piece, cross):
        @pl.when((block // 2 <= place) & (place < line - 1))
        def _():
            upward(block, piece).wait_send()

        @pl.when((block // 2 >= place) & (place > 0))
        def _():
            downward(block, piece).wait_send()

        if cross:
            across(block, piece).wait_send()

    @pl.loop(0, line)
    def _(spot):
        @pl.loop(0, EARLY)
        def _(piece):
            sent(spot * 2 + lane, piece, True)

        @pl.loop(EARLY, CHUNKS)
        def _(piece):
            sent(spot * 2 + lane, piece, False)
            sent(spot * 2 + 1 - lane, piece, False)

    @pl.loop(EARLY, CHUNKS)
    def _(piece):
        across(me, piece).wait_send()


def dense_local(queries, passages, negatives):
    row_count, width = queries.shape
    neg_count = negatives.shape[1]
    owners = lax.axis_size("blk")
    total = owners * row_count
    turned = jnp.pad(negatives.T, ((0, 8 - neg_count), (0, 0)), constant_values=-1)
    out = jax.ShapeDtypeStruct((row_count, width), jnp.bfloat16)
    vmem = pl.BlockSpec(memory_space=pltpu.VMEM)
    anywhere = pl.BlockSpec(memory_space=pl.ANY)
    dma = pltpu.SemaphoreType.DMA
    return pl.pallas_call(
        functools.partial(line_kernel, owners, neg_count),
        out_shape=(out, out),
        in_specs=[anywhere, anywhere, vmem, vmem],
        out_specs=(vmem, vmem),
        scratch_shapes=[
            pltpu.VMEM((2, total, width), jnp.bfloat16),
            pltpu.VMEM((owners, 8, row_count), jnp.int32),
            pltpu.VMEM((2, owners, row_count, row_count), jnp.float32),
            pltpu.VMEM((2, owners, row_count, row_count), jnp.float32),
            pltpu.VMEM((row_count, total), jnp.bfloat16),
            pltpu.VMEM((row_count, total), jnp.bfloat16),
            dma((2,)),
            dma((owners,)),
            dma((owners,)),
            dma((owners, CHUNKS)),
            dma((owners, CHUNKS)),
            dma((owners, CHUNKS)),
            dma((owners, CHUNKS)),
            dma((2,)),
        ],
        compiler_params=pltpu.CompilerParams(
            collective_id=0, has_side_effects=True, vmem_limit_bytes=48 * 1024 * 1024
        ),
        cost_estimate=pl.CostEstimate(
            flops=8 * row_count * total * width,
            bytes_accessed=8 * row_count * width,
            transcendentals=2 * row_count * total,
        ),
    )(queries, passages, negatives, turned)


def solution(mesh):
    owners = mesh.shape["blk"]
    body = dense_local if owners == 8 else local
    return jax.shard_map(
        body,
        mesh=mesh,
        in_specs=(
            P(("groups", "blk"), "sub"),
            P(("groups", "blk"), "sub"),
            P(("groups", "blk"), None),
        ),
        out_specs=(P(("groups", "blk"), "sub"), P(("groups", "blk"), "sub")),
        check_vma=False,
    )
```

```python
import functools
import math

import jax
import jax.numpy as jnp
from jax import lax
from jax.experimental import pallas as pl
from jax.experimental.pallas import tpu as pltpu
from jax.sharding import PartitionSpec as P

D = 4096
HALF = 2


LOGIT_SLOPE = 2.0
LOGIT_SHIFT = -1.0
HARD_WEIGHT = 2.0


def shifted(value, axis, steps):
    count = lax.axis_size(axis)
    pairs = [(source, (source + steps) % count) for source in range(count)]
    return lax.ppermute(value, axis, pairs)


def tile_step(queries, passage_rows, carried, grad_rows, offset, factor):
    partial_value = jnp.einsum(
        "id,jd->ij", queries, passage_rows, preferred_element_type=jnp.float32
    )
    scores = lax.psum(partial_value, "sub")
    weights = jax.nn.sigmoid(factor * scores + LOGIT_SHIFT)
    if offset == 0:
        weights = weights - jnp.eye(weights.shape[0], dtype=jnp.float32)
    coeffs = weights.astype(jnp.bfloat16)
    grad_rows = grad_rows + jnp.dot(coeffs, passage_rows, preferred_element_type=jnp.float32)
    carried = carried + jnp.einsum("ij,id->jd", coeffs, queries, preferred_element_type=jnp.float32)
    return (carried, grad_rows)


def local(queries, passages, negatives):
    factor = LOGIT_SLOPE / math.sqrt(D)
    row_count, width = queries.shape
    zeros_tile = jnp.zeros((row_count, width), jnp.float32)
    grad_rows = zeros_tile
    upper_block = passages
    lower_block = shifted(passages, "blk", 1)
    upper_accum = zeros_tile
    lower_accum = zeros_tile
    for turn_index in range(HALF + 1):
        upper_accum, grad_rows = tile_step(
            queries, upper_block, upper_accum, grad_rows, turn_index, factor
        )
        if turn_index < HALF:
            lower_accum, grad_rows = tile_step(
                queries, lower_block, lower_accum, grad_rows, -(turn_index + 1), factor
            )
            upper_block = shifted(upper_block, "blk", -1)
            upper_accum = shifted(upper_accum, "blk", -1)
        if turn_index < HALF - 1:
            lower_block = shifted(lower_block, "blk", 1)
            lower_accum = shifted(lower_accum.astype(jnp.bfloat16), "blk", 1).astype(
                lower_accum.dtype
            )
    window_pass = shifted(upper_accum, "blk", HALF) + shifted(lower_accum, "blk", -HALF)
    owners = lax.axis_size("blk")
    neg_count = negatives.shape[1]
    capacity = 8 * row_count // owners
    slot_count = row_count * neg_count
    flat_neg = negatives.reshape(-1)
    owner_of = flat_neg // row_count
    local_row = flat_neg % row_count
    onehot_owner = (owner_of[:, None] == jnp.arange(owners, dtype=jnp.int32)[None, :]).astype(
        jnp.int32
    )
    position = jnp.sum((jnp.cumsum(onehot_owner, axis=0) - 1) * onehot_owner, axis=1)
    slot_index = owner_of * capacity + position
    requests = (
        jnp.full((owners * capacity,), -1, jnp.int32)
        .at[slot_index]
        .set(local_row)
        .reshape(owners, capacity)
    )
    incoming = lax.all_to_all(requests, "blk", split_axis=0, concat_axis=0, tiled=True)
    is_live = incoming >= 0
    picked = jnp.where(is_live, incoming, 0)
    rows_out = jnp.take(passages, picked.reshape(-1), axis=0).reshape(owners, capacity, width)
    fetched = lax.all_to_all(rows_out, "blk", split_axis=0, concat_axis=0, tiled=True)
    slot_rows = jnp.take(fetched.reshape(owners * capacity, width), slot_index, axis=0).reshape(
        row_count, neg_count, width
    )
    hard_partial = jnp.einsum("rkd,rd->rk", slot_rows, queries, preferred_element_type=jnp.float32)
    hard_scores = lax.psum(hard_partial, "sub")
    hard_coeffs = (HARD_WEIGHT * jax.nn.sigmoid(factor * hard_scores + LOGIT_SHIFT)).astype(
        jnp.bfloat16
    )
    grad_rows = grad_rows + jnp.einsum(
        "rk,rkd->rd", hard_coeffs, slot_rows, preferred_element_type=jnp.float32
    )
    source_slot = (
        jnp.zeros((owners * capacity,), jnp.int32)
        .at[slot_index]
        .set(jnp.arange(slot_count, dtype=jnp.int32))
    )
    query_buffer = jnp.take(queries, source_slot // neg_count, axis=0).reshape(
        owners, capacity, width
    )
    arrived_rows = lax.all_to_all(query_buffer, "blk", split_axis=0, concat_axis=0, tiled=True)
    owner_partial = jnp.einsum(
        "scd,scd->sc", arrived_rows, rows_out, preferred_element_type=jnp.float32
    )
    owner_scores = lax.psum(owner_partial, "sub")
    owner_coeffs = jnp.where(
        is_live, HARD_WEIGHT * jax.nn.sigmoid(factor * owner_scores + LOGIT_SHIFT), 0.0
    ).astype(jnp.bfloat16)
    member = (
        jnp.arange(row_count, dtype=jnp.int32)[:, None] == picked.reshape(1, -1)
    ) & is_live.reshape(1, -1)
    weighted = jnp.where(member, owner_coeffs.reshape(1, -1), jnp.zeros((), jnp.bfloat16))
    hard_pass = jnp.dot(
        weighted, arrived_rows.reshape(owners * capacity, width), preferred_element_type=jnp.float32
    )
    grad_queries = (factor * grad_rows).astype(jnp.bfloat16)
    grad_passages = (factor * (window_pass + hard_pass)).astype(jnp.bfloat16)
    return (grad_queries, grad_passages)


def pair_weights(scores, counts, near, diagonal, factor):
    gate = jax.nn.sigmoid(factor * scores + LOGIT_SHIFT)
    window = jnp.where(near, gate - diagonal, 0.0).astype(jnp.bfloat16).astype(jnp.float32)
    hard = (HARD_WEIGHT * gate).astype(jnp.bfloat16).astype(jnp.float32)
    return window + counts * hard


PIECES = 4


def grid_kernel(
    owners, neg_count, q_hbm, p_hbm, turned_ref, gq_ref, gp_ref,
    held, pair, turned_all, own_part, other_part, row_w, col_w, part,
    run_up, run_down, got_up, got_down, pass_out, pass_in,
    load_sem, neg_send, neg_recv, pair_sem, swap_send, swap_recv,
    up_send, down_send, held_recv,
    sum_up_send, sum_up_recv, sum_down_send, sum_down_recv, pass_send, pass_recv,
):
    factor = LOGIT_SLOPE / math.sqrt(D)
    row_count, width = q_hbm.shape
    line = owners // 2
    piece_rows = row_count // PIECES
    piece_cols = width // PIECES
    last = line - 1
    me = lax.axis_index("blk")
    side = lax.axis_index("sub")
    place = me // 2
    lane = me % 2
    partner = place * 2 + 1 - lane

    def remote(src, dst, send_sem, recv_sem, target):
        return pltpu.make_async_remote_copy(
            src_ref=src, dst_ref=dst, send_sem=send_sem, recv_sem=recv_sem,
            device_id=target, device_id_type=pl.DeviceIdType.MESH,
        )

    def rows_copy(spot, piece, sems, target):
        rows = pl.ds(pl.multiple_of(piece * piece_rows, piece_rows), piece_rows)
        ref = held.at[spot, rows, :]
        return remote(ref, ref, sems.at[spot, piece], held_recv.at[spot, piece], {"blk": target})

    def rows_up(spot, piece):
        return rows_copy(spot, piece, up_send, me + 2)

    def rows_down(spot, piece):
        return rows_copy(spot, piece, down_send, me - 2)

    def sum_up(spot, piece):
        return remote(
            run_up.at[spot, piece], got_up.at[spot, piece],
            sum_up_send.at[spot, piece], sum_up_recv.at[spot, piece], {"blk": me + 2},
        )

    def sum_down(spot, piece):
        return remote(
            run_down.at[spot, piece], got_down.at[spot, piece],
            sum_down_send.at[spot, piece], sum_down_recv.at[spot, piece], {"blk": me - 2},
        )

    def pass_copy(piece):
        return remote(
            pass_out.at[piece], pass_in.at[piece],
            pass_send.at[piece], pass_recv.at[piece], {"blk": partner},
        )

    def pair_copy(which):
        return remote(
            pair.at[which], pair.at[which], pair_sem.at[0], pair_sem.at[1], {"blk": partner}
        )

    def swap(spot):
        return remote(
            own_part.at[spot], other_part.at[spot],
            swap_send.at[spot], swap_recv.at[spot], {"sub": 1 - side},
        )

    def neg_copy(step, spot):
        target = ((place + step) % line) * 2 + lane
        return remote(
            turned_all.at[spot], turned_all.at[spot],
            neg_send.at[step], neg_recv.at[spot], {"blk": target},
        )

    loads = [
        pltpu.make_async_copy(q_hbm, held.at[place], load_sem.at[0]),
        pltpu.make_async_copy(p_hbm, pair.at[lane], load_sem.at[1]),
    ]
    for load in loads:
        load.start()
    barrier = pltpu.get_barrier_semaphore()
    for step in range(1, line):
        pl.semaphore_signal(
            barrier, inc=1, device_id={"blk": ((place + step) % line) * 2 + lane},
            device_id_type=pl.DeviceIdType.MESH,
        )
    pl.semaphore_signal(
        barrier, inc=1, device_id={"blk": partner}, device_id_type=pl.DeviceIdType.MESH
    )
    pl.semaphore_signal(
        barrier, inc=1, device_id={"sub": 1 - side}, device_id_type=pl.DeviceIdType.MESH
    )
    turned_all[place] = turned_ref[...]
    for load in loads:
        load.wait()
    pl.semaphore_wait(barrier, line + 1)

    pair_copy(lane).start()

    @pl.loop(0, PIECES)
    def _(piece):
        @pl.when(place < last)
        def _():
            rows_up(place, piece).start()

        @pl.when(place > 0)
        def _():
            rows_down(place, piece).start()

    for step in range(1, line):
        neg_copy(step, place).start()

    down_index = lax.broadcasted_iota(jnp.int32, (row_count, row_count), 0)
    across_index = lax.broadcasted_iota(jnp.int32, (row_count, row_count), 1)

    def score(spot):
        own_part[spot] = lax.dot_general(
            pair[...].reshape(2 * row_count, width), held[spot], (((1,), (1,)), ((), ())),
            preferred_element_type=jnp.float32,
        )
        swap(spot).start()

    def product(spot):
        swap(spot).wait()
        query_block = spot * 2 + lane
        for which in range(2):
            passage_block = place * 2 + which
            gap = (passage_block - query_block + HALF + owners) % owners
            near = (jnp.zeros((row_count, row_count), jnp.int32) + gap) <= 2 * HALF
            passage = down_index + passage_block * row_count
            diagonal = (passage == across_index + query_block * row_count).astype(jnp.float32)
            counts = jnp.zeros((row_count, row_count), jnp.float32)
            for k in range(neg_count):
                counts += (turned_all[spot, k : k + 1, :] == passage).astype(jnp.float32)
            rows = slice(which * row_count, (which + 1) * row_count)
            weights = pair_weights(
                own_part[spot, rows] + other_part[spot, rows], counts, near, diagonal, factor
            )
            columns = pl.ds(pl.multiple_of(spot * row_count, row_count), row_count)
            col_w[which, :, columns] = weights.astype(jnp.bfloat16)
            row_w[:, rows] = weights.T.astype(jnp.bfloat16)

        for piece in range(PIECES):
            columns = slice(piece * piece_cols, (piece + 1) * piece_cols)
            part[spot, piece] = jnp.dot(
                row_w[...], pair[:, :, columns].reshape(2 * row_count, piece_cols),
                preferred_element_type=jnp.float32,
            )

    def passage_sum(which, piece):
        columns = pl.ds(pl.multiple_of(piece * piece_cols, piece_cols), piece_cols)
        return jnp.dot(
            col_w[which], held[:, :, columns].reshape(line * row_count, piece_cols),
            preferred_element_type=jnp.float32,
        )

    def send_passage_sums():
        @pl.loop(0, PIECES)
        def _(piece):
            pass_out[piece] = passage_sum(1 - lane, piece).astype(jnp.bfloat16)
            pass_copy(piece).start()

    for far in range(1, line):
        @pl.loop(0, PIECES)
        def _(piece):
            @pl.when(place >= far)
            def _():
                rows_up(place - far, piece).wait_recv()

                @pl.when(place < last)
                def _():
                    rows_up(place - far, piece).start()

            @pl.when(place + far < line)
            def _():
                rows_down(place + far, piece).wait_recv()

                @pl.when(place > 0)
                def _():
                    rows_down(place + far, piece).start()

        if far == 1:
            pair_copy(1 - lane).wait_recv()

        below = place - far
        above = place + far
        for spot, ready in ((below, place >= far), (above, place + far < line)):
            @pl.when(ready)
            def _():
                score(spot)

        for spot, ready in ((below, place >= far), (above, place + far < line)):
            @pl.when(ready)
            def _():
                neg_copy(1, spot).wait_recv()
                product(spot)

        inner = (place > 0) & (place < last)
        if far == line - 1:
            @pl.when(inner)
            def _():
                send_passage_sums()

        @pl.loop(0, PIECES)
        def _(piece):
            @pl.when(place < far)
            def _():
                @pl.when(place == 0)
                def _():
                    run_up[far, piece] = part[far, piece].astype(jnp.bfloat16)

                @pl.when(place > 0)
                def _():
                    sum_up(far, piece).wait_recv()
                    run_up[far, piece] = (
                        part[far, piece] + got_up[far, piece].astype(jnp.float32)
                    ).astype(jnp.bfloat16)

                sum_up(far, piece).start()

            spot = last - far

            @pl.when(place > spot)
            def _():
                @pl.when(place == last)
                def _():
                    run_down[spot, piece] = part[spot, piece].astype(jnp.bfloat16)

                @pl.when(place < last)
                def _():
                    sum_down(spot, piece).wait_recv()
                    run_down[spot, piece] = (
                        part[spot, piece] + got_down[spot, piece].astype(jnp.float32)
                    ).astype(jnp.bfloat16)

                sum_down(spot, piece).start()

        if far == 1:
            score(place)
            product(place)

        if far == line - 1:
            @pl.when(jnp.logical_not(inner))
            def _():
                send_passage_sums()

    @pl.loop(0, PIECES)
    def _(piece):
        columns = pl.ds(pl.multiple_of(piece * piece_cols, piece_cols), piece_cols)

        @pl.when(place > 0)
        def _():
            sum_up(place, piece).wait_recv()
            part[place, piece] += got_up[place, piece].astype(jnp.float32)

        @pl.when(place < last)
        def _():
            sum_down(place, piece).wait_recv()
            part[place, piece] += got_down[place, piece].astype(jnp.float32)

        gq_ref[:, columns] = (factor * part[place, piece]).astype(jnp.bfloat16)

    @pl.loop(0, PIECES)
    def _(piece):
        columns = pl.ds(pl.multiple_of(piece * piece_cols, piece_cols), piece_cols)
        mine = passage_sum(lane, piece)
        pass_copy(piece).wait_recv()
        gp_ref[:, columns] = (
            factor * (mine + pass_in[piece].astype(jnp.float32))
        ).astype(jnp.bfloat16)

    pair_copy(lane).wait_send()
    for step in range(1, line):
        neg_copy(step, place).wait_send()

    @pl.loop(0, PIECES)
    def _(piece):
        pass_copy(piece).wait_send()
        for spot in range(line):
            @pl.when((place >= spot) & (place < last))
            def _():
                rows_up(spot, piece).wait_send()

            @pl.when((place <= spot) & (place > 0))
            def _():
                rows_down(spot, piece).wait_send()

            @pl.when(place < spot)
            def _():
                sum_up(spot, piece).wait_send()

            @pl.when(place > spot)
            def _():
                sum_down(spot, piece).wait_send()


def dense_local(queries, passages, negatives):
    row_count, width = queries.shape
    neg_count = negatives.shape[1]
    owners = lax.axis_size("blk")
    line = owners // 2
    piece_cols = width // PIECES
    turned = jnp.pad(negatives.T, ((0, 8 - neg_count), (0, 0)), constant_values=-1)
    out = jax.ShapeDtypeStruct((row_count, width), jnp.bfloat16)
    vmem = pl.BlockSpec(memory_space=pltpu.VMEM)
    anywhere = pl.BlockSpec(memory_space=pl.ANY)
    dma = pltpu.SemaphoreType.DMA
    sums = pltpu.VMEM((line, PIECES, row_count, piece_cols), jnp.bfloat16)
    grid = dma((line, PIECES))
    return pl.pallas_call(
        functools.partial(grid_kernel, owners, neg_count),
        out_shape=(out, out),
        in_specs=[anywhere, anywhere, vmem],
        out_specs=(vmem, vmem),
        scratch_shapes=[
            pltpu.VMEM((line, row_count, width), jnp.bfloat16),
            pltpu.VMEM((2, row_count, width), jnp.bfloat16),
            pltpu.VMEM((line, 8, row_count), jnp.int32),
            pltpu.VMEM((line, 2 * row_count, row_count), jnp.float32),
            pltpu.VMEM((line, 2 * row_count, row_count), jnp.float32),
            pltpu.VMEM((row_count, 2 * row_count), jnp.bfloat16),
            pltpu.VMEM((2, row_count, line * row_count), jnp.bfloat16),
            pltpu.VMEM((line, PIECES, row_count, piece_cols), jnp.float32),
            sums,
            sums,
            sums,
            sums,
            pltpu.VMEM((PIECES, row_count, piece_cols), jnp.bfloat16),
            pltpu.VMEM((PIECES, row_count, piece_cols), jnp.bfloat16),
            dma((2,)),
            dma((line,)),
            dma((line,)),
            dma((2,)),
            dma((line,)),
            dma((line,)),
            grid,
            grid,
            grid,
            grid,
            grid,
            grid,
            grid,
            dma((PIECES,)),
            dma((PIECES,)),
        ],
        compiler_params=pltpu.CompilerParams(
            collective_id=0, has_side_effects=True, vmem_limit_bytes=60 * 1024 * 1024
        ),
        cost_estimate=pl.CostEstimate(
            flops=12 * row_count * row_count * owners * width // 2,
            bytes_accessed=8 * row_count * width,
            transcendentals=row_count * row_count * owners,
        ),
    )(queries, passages, turned)


def solution(mesh):
    owners = mesh.shape["blk"]
    body = dense_local if owners == 8 else local
    return jax.shard_map(
        body,
        mesh=mesh,
        in_specs=(
            P(("groups", "blk"), "sub"),
            P(("groups", "blk"), "sub"),
            P(("groups", "blk"), None),
        ),
        out_specs=(P(("groups", "blk"), "sub"), P(("groups", "blk"), "sub")),
        check_vma=False,
    )
```

```python
import functools
import math

import jax
import jax.numpy as jnp
from jax import lax
from jax.experimental import pallas as pl
from jax.experimental.pallas import tpu as pltpu
from jax.sharding import PartitionSpec as P

D = 4096
HALF = 2


LOGIT_SLOPE = 2.0
LOGIT_SHIFT = -1.0
HARD_WEIGHT = 2.0


def shifted(value, axis, steps):
    count = lax.axis_size(axis)
    pairs = [(source, (source + steps) % count) for source in range(count)]
    return lax.ppermute(value, axis, pairs)


def tile_step(queries, passage_rows, carried, grad_rows, offset, factor):
    partial_value = jnp.einsum(
        "id,jd->ij", queries, passage_rows, preferred_element_type=jnp.float32
    )
    scores = lax.psum(partial_value, "sub")
    weights = jax.nn.sigmoid(factor * scores + LOGIT_SHIFT)
    if offset == 0:
        weights = weights - jnp.eye(weights.shape[0], dtype=jnp.float32)
    coeffs = weights.astype(jnp.bfloat16)
    grad_rows = grad_rows + jnp.dot(coeffs, passage_rows, preferred_element_type=jnp.float32)
    carried = carried + jnp.einsum("ij,id->jd", coeffs, queries, preferred_element_type=jnp.float32)
    return (carried, grad_rows)


def local(queries, passages, negatives):
    factor = LOGIT_SLOPE / math.sqrt(D)
    row_count, width = queries.shape
    zeros_tile = jnp.zeros((row_count, width), jnp.float32)
    grad_rows = zeros_tile
    upper_block = passages
    lower_block = shifted(passages, "blk", 1)
    upper_accum = zeros_tile
    lower_accum = zeros_tile
    for turn_index in range(HALF + 1):
        upper_accum, grad_rows = tile_step(
            queries, upper_block, upper_accum, grad_rows, turn_index, factor
        )
        if turn_index < HALF:
            lower_accum, grad_rows = tile_step(
                queries, lower_block, lower_accum, grad_rows, -(turn_index + 1), factor
            )
            upper_block = shifted(upper_block, "blk", -1)
            upper_accum = shifted(upper_accum, "blk", -1)
        if turn_index < HALF - 1:
            lower_block = shifted(lower_block, "blk", 1)
            lower_accum = shifted(lower_accum.astype(jnp.bfloat16), "blk", 1).astype(
                lower_accum.dtype
            )
    window_pass = shifted(upper_accum, "blk", HALF) + shifted(lower_accum, "blk", -HALF)
    owners = lax.axis_size("blk")
    neg_count = negatives.shape[1]
    capacity = 8 * row_count // owners
    slot_count = row_count * neg_count
    flat_neg = negatives.reshape(-1)
    owner_of = flat_neg // row_count
    local_row = flat_neg % row_count
    onehot_owner = (owner_of[:, None] == jnp.arange(owners, dtype=jnp.int32)[None, :]).astype(
        jnp.int32
    )
    position = jnp.sum((jnp.cumsum(onehot_owner, axis=0) - 1) * onehot_owner, axis=1)
    slot_index = owner_of * capacity + position
    requests = (
        jnp.full((owners * capacity,), -1, jnp.int32)
        .at[slot_index]
        .set(local_row)
        .reshape(owners, capacity)
    )
    incoming = lax.all_to_all(requests, "blk", split_axis=0, concat_axis=0, tiled=True)
    is_live = incoming >= 0
    picked = jnp.where(is_live, incoming, 0)
    rows_out = jnp.take(passages, picked.reshape(-1), axis=0).reshape(owners, capacity, width)
    fetched = lax.all_to_all(rows_out, "blk", split_axis=0, concat_axis=0, tiled=True)
    slot_rows = jnp.take(fetched.reshape(owners * capacity, width), slot_index, axis=0).reshape(
        row_count, neg_count, width
    )
    hard_partial = jnp.einsum("rkd,rd->rk", slot_rows, queries, preferred_element_type=jnp.float32)
    hard_scores = lax.psum(hard_partial, "sub")
    hard_coeffs = (HARD_WEIGHT * jax.nn.sigmoid(factor * hard_scores + LOGIT_SHIFT)).astype(
        jnp.bfloat16
    )
    grad_rows = grad_rows + jnp.einsum(
        "rk,rkd->rd", hard_coeffs, slot_rows, preferred_element_type=jnp.float32
    )
    source_slot = (
        jnp.zeros((owners * capacity,), jnp.int32)
        .at[slot_index]
        .set(jnp.arange(slot_count, dtype=jnp.int32))
    )
    query_buffer = jnp.take(queries, source_slot // neg_count, axis=0).reshape(
        owners, capacity, width
    )
    arrived_rows = lax.all_to_all(query_buffer, "blk", split_axis=0, concat_axis=0, tiled=True)
    owner_partial = jnp.einsum(
        "scd,scd->sc", arrived_rows, rows_out, preferred_element_type=jnp.float32
    )
    owner_scores = lax.psum(owner_partial, "sub")
    owner_coeffs = jnp.where(
        is_live, HARD_WEIGHT * jax.nn.sigmoid(factor * owner_scores + LOGIT_SHIFT), 0.0
    ).astype(jnp.bfloat16)
    member = (
        jnp.arange(row_count, dtype=jnp.int32)[:, None] == picked.reshape(1, -1)
    ) & is_live.reshape(1, -1)
    weighted = jnp.where(member, owner_coeffs.reshape(1, -1), jnp.zeros((), jnp.bfloat16))
    hard_pass = jnp.dot(
        weighted, arrived_rows.reshape(owners * capacity, width), preferred_element_type=jnp.float32
    )
    grad_queries = (factor * grad_rows).astype(jnp.bfloat16)
    grad_passages = (factor * (window_pass + hard_pass)).astype(jnp.bfloat16)
    return (grad_queries, grad_passages)


def pair_weights(scores, counts, near, diagonal, factor):
    gate = jax.nn.sigmoid(factor * scores + LOGIT_SHIFT)
    window = jnp.where(near, gate - diagonal, 0.0).astype(jnp.bfloat16).astype(jnp.float32)
    hard = (HARD_WEIGHT * gate).astype(jnp.bfloat16).astype(jnp.float32)
    return window + counts * hard


PIECES = 4
ROW_PIECES = 4
LAG = 1


def grid_kernel(
    owners, neg_count, q_hbm, p_hbm, turned_ref, gq_ref, gp_ref,
    held, pair, turned_all, own_part, other_part, row_w, col_w, part,
    run_up, run_down, got_up, got_down, pass_out, pass_in,
    load_sem, neg_send, neg_recv, pair_sem, swap_send, swap_recv,
    up_send, down_send, held_recv,
    sum_up_send, sum_up_recv, sum_down_send, sum_down_recv, pass_send, pass_recv,
):
    factor = LOGIT_SLOPE / math.sqrt(D)
    row_count, width = q_hbm.shape
    line = owners // 2
    piece_rows = row_count // ROW_PIECES
    piece_cols = width // PIECES
    last = line - 1
    me = lax.axis_index("blk")
    side = lax.axis_index("sub")
    place = me // 2
    lane = me % 2
    partner = place * 2 + 1 - lane

    def remote(src, dst, send_sem, recv_sem, target):
        return pltpu.make_async_remote_copy(
            src_ref=src, dst_ref=dst, send_sem=send_sem, recv_sem=recv_sem,
            device_id=target, device_id_type=pl.DeviceIdType.MESH,
        )

    def rows_copy(spot, piece, sems, target):
        rows = pl.ds(pl.multiple_of(piece * piece_rows, piece_rows), piece_rows)
        ref = held.at[spot, rows, :]
        return remote(ref, ref, sems.at[spot, piece], held_recv.at[spot, piece], {"blk": target})

    def rows_up(spot, piece):
        return rows_copy(spot, piece, up_send, me + 2)

    def rows_down(spot, piece):
        return rows_copy(spot, piece, down_send, me - 2)

    def sum_up(spot, piece):
        return remote(
            run_up.at[spot, piece], got_up.at[spot, piece],
            sum_up_send.at[spot, piece], sum_up_recv.at[spot, piece], {"blk": me + 2},
        )

    def sum_down(spot, piece):
        return remote(
            run_down.at[spot, piece], got_down.at[spot, piece],
            sum_down_send.at[spot, piece], sum_down_recv.at[spot, piece], {"blk": me - 2},
        )

    def pass_copy(piece):
        return remote(
            pass_out.at[piece], pass_in.at[piece],
            pass_send.at[piece], pass_recv.at[piece], {"blk": partner},
        )

    def pair_copy(which):
        return remote(
            pair.at[which], pair.at[which], pair_sem.at[0], pair_sem.at[1], {"blk": partner}
        )

    def swap(spot):
        return remote(
            own_part.at[spot], other_part.at[spot],
            swap_send.at[spot], swap_recv.at[spot], {"sub": 1 - side},
        )

    def neg_copy(step, spot):
        target = ((place + step) % line) * 2 + lane
        return remote(
            turned_all.at[spot], turned_all.at[spot],
            neg_send.at[step], neg_recv.at[spot], {"blk": target},
        )

    loads = [
        pltpu.make_async_copy(q_hbm, held.at[place], load_sem.at[0]),
        pltpu.make_async_copy(p_hbm, pair.at[lane], load_sem.at[1]),
    ]
    for load in loads:
        load.start()
    barrier = pltpu.get_barrier_semaphore()
    for step in range(1, line):
        pl.semaphore_signal(
            barrier, inc=1, device_id={"blk": ((place + step) % line) * 2 + lane},
            device_id_type=pl.DeviceIdType.MESH,
        )
    pl.semaphore_signal(
        barrier, inc=1, device_id={"blk": partner}, device_id_type=pl.DeviceIdType.MESH
    )
    pl.semaphore_signal(
        barrier, inc=1, device_id={"sub": 1 - side}, device_id_type=pl.DeviceIdType.MESH
    )
    turned_all[place] = turned_ref[...]
    for load in loads:
        load.wait()
    pl.semaphore_wait(barrier, line + 1)

    pair_copy(lane).start()

    @pl.loop(0, ROW_PIECES)
    def _(piece):
        @pl.when(place < last)
        def _():
            rows_up(place, piece).start()

        @pl.when(place > 0)
        def _():
            rows_down(place, piece).start()

    for step in range(1, line):
        neg_copy(step, place).start()

    down_index = lax.broadcasted_iota(jnp.int32, (row_count, row_count), 0)
    across_index = lax.broadcasted_iota(jnp.int32, (row_count, row_count), 1)

    def score(spot):
        own_part[spot] = lax.dot_general(
            pair[...].reshape(2 * row_count, width), held[spot], (((1,), (1,)), ((), ())),
            preferred_element_type=jnp.float32,
        )
        swap(spot).start()

    def product(spot):
        swap(spot).wait()
        query_block = spot * 2 + lane
        for which in range(2):
            passage_block = place * 2 + which
            gap = (passage_block - query_block + HALF + owners) % owners
            near = (jnp.zeros((row_count, row_count), jnp.int32) + gap) <= 2 * HALF
            passage = down_index + passage_block * row_count
            diagonal = (passage == across_index + query_block * row_count).astype(jnp.float32)
            counts = jnp.zeros((row_count, row_count), jnp.float32)
            for k in range(neg_count):
                counts += (turned_all[spot, k : k + 1, :] == passage).astype(jnp.float32)
            rows = slice(which * row_count, (which + 1) * row_count)
            weights = pair_weights(
                own_part[spot, rows] + other_part[spot, rows], counts, near, diagonal, factor
            )
            columns = pl.ds(pl.multiple_of(spot * row_count, row_count), row_count)
            col_w[which, :, columns] = weights.astype(jnp.bfloat16)
            row_w[:, rows] = weights.T.astype(jnp.bfloat16)

        for piece in range(PIECES):
            columns = slice(piece * piece_cols, (piece + 1) * piece_cols)
            part[spot, piece] = jnp.dot(
                row_w[...], pair[:, :, columns].reshape(2 * row_count, piece_cols),
                preferred_element_type=jnp.float32,
            )

    def passage_sum(which, piece):
        columns = pl.ds(pl.multiple_of(piece * piece_cols, piece_cols), piece_cols)
        return jnp.dot(
            col_w[which], held[:, :, columns].reshape(line * row_count, piece_cols),
            preferred_element_type=jnp.float32,
        )

    def send_passage_sums():
        @pl.loop(0, PIECES)
        def _(piece):
            pass_out[piece] = passage_sum(1 - lane, piece).astype(jnp.bfloat16)
            pass_copy(piece).start()

    for far in range(1, line):
        @pl.loop(0, ROW_PIECES)
        def _(piece):
            @pl.when(place >= far)
            def _():
                rows_up(place - far, piece).wait_recv()

                @pl.when(place < last)
                def _():
                    rows_up(place - far, piece).start()

            @pl.when(place + far < line)
            def _():
                rows_down(place + far, piece).wait_recv()

                @pl.when(place > 0)
                def _():
                    rows_down(place + far, piece).start()

        if far == 1:
            pair_copy(1 - lane).wait_recv()

        below = place - far
        above = place + far
        for spot, ready in ((below, place >= far), (above, place + far < line)):
            @pl.when(ready)
            def _():
                score(spot)

        for spot, ready in ((below, place >= far), (above, place + far < line)):
            @pl.when(ready)
            def _():
                neg_copy(1, spot).wait_recv()
                product(spot)

        inner = (place > 0) & (place < last)
        if far == line - 2:
            @pl.when(inner)
            def _():
                send_passage_sums()

        spot = last - far
        low = place * 2 < line

        @pl.loop(0, PIECES + LAG)
        def _(step):
            piece = step - jnp.where(low, 0, LAG)

            @pl.when((place < far) & (piece >= 0) & (piece < PIECES))
            def _():
                @pl.when(place == 0)
                def _():
                    run_up[far, piece] = part[far, piece].astype(jnp.bfloat16)

                @pl.when(place > 0)
                def _():
                    sum_up(far, piece).wait_recv()
                    run_up[far, piece] = (
                        part[far, piece] + got_up[far, piece].astype(jnp.float32)
                    ).astype(jnp.bfloat16)

                sum_up(far, piece).start()

            other = step - jnp.where(low, LAG, 0)

            @pl.when((place > spot) & (other >= 0) & (other < PIECES))
            def _():
                @pl.when(place == last)
                def _():
                    run_down[spot, other] = part[spot, other].astype(jnp.bfloat16)

                @pl.when(place < last)
                def _():
                    sum_down(spot, other).wait_recv()
                    run_down[spot, other] = (
                        part[spot, other] + got_down[spot, other].astype(jnp.float32)
                    ).astype(jnp.bfloat16)

                sum_down(spot, other).start()

        if far == 1:
            score(place)
            product(place)

        if far == line - 1:
            @pl.when(jnp.logical_not(inner))
            def _():
                send_passage_sums()

    @pl.loop(0, PIECES)
    def _(piece):
        columns = pl.ds(pl.multiple_of(piece * piece_cols, piece_cols), piece_cols)

        @pl.when(place > 0)
        def _():
            sum_up(place, piece).wait_recv()
            part[place, piece] += got_up[place, piece].astype(jnp.float32)

        @pl.when(place < last)
        def _():
            sum_down(place, piece).wait_recv()
            part[place, piece] += got_down[place, piece].astype(jnp.float32)

        gq_ref[:, columns] = (factor * part[place, piece]).astype(jnp.bfloat16)

    @pl.loop(0, PIECES)
    def _(piece):
        columns = pl.ds(pl.multiple_of(piece * piece_cols, piece_cols), piece_cols)
        mine = passage_sum(lane, piece)
        pass_copy(piece).wait_recv()
        gp_ref[:, columns] = (
            factor * (mine + pass_in[piece].astype(jnp.float32))
        ).astype(jnp.bfloat16)

    pair_copy(lane).wait_send()
    for step in range(1, line):
        neg_copy(step, place).wait_send()

    @pl.loop(0, ROW_PIECES)
    def _(piece):
        for spot in range(line):
            @pl.when((place >= spot) & (place < last))
            def _():
                rows_up(spot, piece).wait_send()

            @pl.when((place <= spot) & (place > 0))
            def _():
                rows_down(spot, piece).wait_send()

    @pl.loop(0, PIECES)
    def _(piece):
        pass_copy(piece).wait_send()
        for spot in range(line):
            @pl.when(place < spot)
            def _():
                sum_up(spot, piece).wait_send()

            @pl.when(place > spot)
            def _():
                sum_down(spot, piece).wait_send()


def dense_local(queries, passages, negatives):
    row_count, width = queries.shape
    neg_count = negatives.shape[1]
    owners = lax.axis_size("blk")
    line = owners // 2
    piece_cols = width // PIECES
    turned = jnp.pad(negatives.T, ((0, 8 - neg_count), (0, 0)), constant_values=-1)
    out = jax.ShapeDtypeStruct((row_count, width), jnp.bfloat16)
    vmem = pl.BlockSpec(memory_space=pltpu.VMEM)
    anywhere = pl.BlockSpec(memory_space=pl.ANY)
    dma = pltpu.SemaphoreType.DMA
    sums = pltpu.VMEM((line, PIECES, row_count, piece_cols), jnp.bfloat16)
    grid = dma((line, PIECES))
    row_grid = dma((line, ROW_PIECES))
    return pl.pallas_call(
        functools.partial(grid_kernel, owners, neg_count),
        out_shape=(out, out),
        in_specs=[anywhere, anywhere, vmem],
        out_specs=(vmem, vmem),
        scratch_shapes=[
            pltpu.VMEM((line, row_count, width), jnp.bfloat16),
            pltpu.VMEM((2, row_count, width), jnp.bfloat16),
            pltpu.VMEM((line, 8, row_count), jnp.int32),
            pltpu.VMEM((line, 2 * row_count, row_count), jnp.float32),
            pltpu.VMEM((line, 2 * row_count, row_count), jnp.float32),
            pltpu.VMEM((row_count, 2 * row_count), jnp.bfloat16),
            pltpu.VMEM((2, row_count, line * row_count), jnp.bfloat16),
            pltpu.VMEM((line, PIECES, row_count, piece_cols), jnp.float32),
            sums,
            sums,
            sums,
            sums,
            pltpu.VMEM((PIECES, row_count, piece_cols), jnp.bfloat16),
            pltpu.VMEM((PIECES, row_count, piece_cols), jnp.bfloat16),
            dma((2,)),
            dma((line,)),
            dma((line,)),
            dma((2,)),
            dma((line,)),
            dma((line,)),
            row_grid,
            row_grid,
            row_grid,
            grid,
            grid,
            grid,
            grid,
            dma((PIECES,)),
            dma((PIECES,)),
        ],
        compiler_params=pltpu.CompilerParams(
            collective_id=0, has_side_effects=True, vmem_limit_bytes=60 * 1024 * 1024
        ),
        cost_estimate=pl.CostEstimate(
            flops=12 * row_count * row_count * owners * width // 2,
            bytes_accessed=8 * row_count * width,
            transcendentals=row_count * row_count * owners,
        ),
    )(queries, passages, turned)


def solution(mesh):
    owners = mesh.shape["blk"]
    body = dense_local if owners == 8 else local
    return jax.shard_map(
        body,
        mesh=mesh,
        in_specs=(
            P(("groups", "blk"), "sub"),
            P(("groups", "blk"), "sub"),
            P(("groups", "blk"), None),
        ),
        out_specs=(P(("groups", "blk"), "sub"), P(("groups", "blk"), "sub")),
        check_vma=False,
    )
```

```python
import functools
import math

import jax
import jax.numpy as jnp
from jax import lax
from jax.experimental import pallas as pl
from jax.experimental.pallas import tpu as pltpu
from jax.sharding import PartitionSpec as P

D = 4096
HALF = 2


LOGIT_SLOPE = 2.0
LOGIT_SHIFT = -1.0
HARD_WEIGHT = 2.0


def shifted(value, axis, steps):
    count = lax.axis_size(axis)
    pairs = [(source, (source + steps) % count) for source in range(count)]
    return lax.ppermute(value, axis, pairs)


def tile_step(queries, passage_rows, carried, grad_rows, offset, factor):
    partial_value = jnp.einsum(
        "id,jd->ij", queries, passage_rows, preferred_element_type=jnp.float32
    )
    scores = lax.psum(partial_value, "sub")
    weights = jax.nn.sigmoid(factor * scores + LOGIT_SHIFT)
    if offset == 0:
        weights = weights - jnp.eye(weights.shape[0], dtype=jnp.float32)
    coeffs = weights.astype(jnp.bfloat16)
    grad_rows = grad_rows + jnp.dot(coeffs, passage_rows, preferred_element_type=jnp.float32)
    carried = carried + jnp.einsum("ij,id->jd", coeffs, queries, preferred_element_type=jnp.float32)
    return (carried, grad_rows)


def local(queries, passages, negatives):
    factor = LOGIT_SLOPE / math.sqrt(D)
    row_count, width = queries.shape
    zeros_tile = jnp.zeros((row_count, width), jnp.float32)
    grad_rows = zeros_tile
    upper_block = passages
    lower_block = shifted(passages, "blk", 1)
    upper_accum = zeros_tile
    lower_accum = zeros_tile
    for turn_index in range(HALF + 1):
        upper_accum, grad_rows = tile_step(
            queries, upper_block, upper_accum, grad_rows, turn_index, factor
        )
        if turn_index < HALF:
            lower_accum, grad_rows = tile_step(
                queries, lower_block, lower_accum, grad_rows, -(turn_index + 1), factor
            )
            upper_block = shifted(upper_block, "blk", -1)
            upper_accum = shifted(upper_accum, "blk", -1)
        if turn_index < HALF - 1:
            lower_block = shifted(lower_block, "blk", 1)
            lower_accum = shifted(lower_accum.astype(jnp.bfloat16), "blk", 1).astype(
                lower_accum.dtype
            )
    window_pass = shifted(upper_accum, "blk", HALF) + shifted(lower_accum, "blk", -HALF)
    owners = lax.axis_size("blk")
    neg_count = negatives.shape[1]
    capacity = 8 * row_count // owners
    slot_count = row_count * neg_count
    flat_neg = negatives.reshape(-1)
    owner_of = flat_neg // row_count
    local_row = flat_neg % row_count
    onehot_owner = (owner_of[:, None] == jnp.arange(owners, dtype=jnp.int32)[None, :]).astype(
        jnp.int32
    )
    position = jnp.sum((jnp.cumsum(onehot_owner, axis=0) - 1) * onehot_owner, axis=1)
    slot_index = owner_of * capacity + position
    requests = (
        jnp.full((owners * capacity,), -1, jnp.int32)
        .at[slot_index]
        .set(local_row)
        .reshape(owners, capacity)
    )
    incoming = lax.all_to_all(requests, "blk", split_axis=0, concat_axis=0, tiled=True)
    is_live = incoming >= 0
    picked = jnp.where(is_live, incoming, 0)
    rows_out = jnp.take(passages, picked.reshape(-1), axis=0).reshape(owners, capacity, width)
    fetched = lax.all_to_all(rows_out, "blk", split_axis=0, concat_axis=0, tiled=True)
    slot_rows = jnp.take(fetched.reshape(owners * capacity, width), slot_index, axis=0).reshape(
        row_count, neg_count, width
    )
    hard_partial = jnp.einsum("rkd,rd->rk", slot_rows, queries, preferred_element_type=jnp.float32)
    hard_scores = lax.psum(hard_partial, "sub")
    hard_coeffs = (HARD_WEIGHT * jax.nn.sigmoid(factor * hard_scores + LOGIT_SHIFT)).astype(
        jnp.bfloat16
    )
    grad_rows = grad_rows + jnp.einsum(
        "rk,rkd->rd", hard_coeffs, slot_rows, preferred_element_type=jnp.float32
    )
    source_slot = (
        jnp.zeros((owners * capacity,), jnp.int32)
        .at[slot_index]
        .set(jnp.arange(slot_count, dtype=jnp.int32))
    )
    query_buffer = jnp.take(queries, source_slot // neg_count, axis=0).reshape(
        owners, capacity, width
    )
    arrived_rows = lax.all_to_all(query_buffer, "blk", split_axis=0, concat_axis=0, tiled=True)
    owner_partial = jnp.einsum(
        "scd,scd->sc", arrived_rows, rows_out, preferred_element_type=jnp.float32
    )
    owner_scores = lax.psum(owner_partial, "sub")
    owner_coeffs = jnp.where(
        is_live, HARD_WEIGHT * jax.nn.sigmoid(factor * owner_scores + LOGIT_SHIFT), 0.0
    ).astype(jnp.bfloat16)
    member = (
        jnp.arange(row_count, dtype=jnp.int32)[:, None] == picked.reshape(1, -1)
    ) & is_live.reshape(1, -1)
    weighted = jnp.where(member, owner_coeffs.reshape(1, -1), jnp.zeros((), jnp.bfloat16))
    hard_pass = jnp.dot(
        weighted, arrived_rows.reshape(owners * capacity, width), preferred_element_type=jnp.float32
    )
    grad_queries = (factor * grad_rows).astype(jnp.bfloat16)
    grad_passages = (factor * (window_pass + hard_pass)).astype(jnp.bfloat16)
    return (grad_queries, grad_passages)


def pair_weights(scores, counts, near, diagonal, factor):
    gate = jax.nn.sigmoid(factor * scores + LOGIT_SHIFT)
    window = jnp.where(near, gate - diagonal, 0.0).astype(jnp.bfloat16).astype(jnp.float32)
    hard = (HARD_WEIGHT * gate).astype(jnp.bfloat16).astype(jnp.float32)
    return window + counts * hard


PIECES = 8
ROW_PIECES = 4
LAG = 2


def grid_kernel(
    owners, neg_count, q_hbm, p_hbm, turned_ref, gq_ref, gp_ref,
    held, pair, turned_all, own_part, other_part, row_w, col_w, part,
    run_up, run_down, got_up, got_down, pass_out, pass_in,
    load_sem, neg_send, neg_recv, pair_sem, swap_send, swap_recv,
    up_send, down_send, held_recv,
    sum_up_send, sum_up_recv, sum_down_send, sum_down_recv, pass_send, pass_recv,
):
    factor = LOGIT_SLOPE / math.sqrt(D)
    row_count, width = q_hbm.shape
    line = owners // 2
    piece_rows = row_count // ROW_PIECES
    piece_cols = width // PIECES
    last = line - 1
    me = lax.axis_index("blk")
    side = lax.axis_index("sub")
    place = me // 2
    lane = me % 2
    partner = place * 2 + 1 - lane

    def remote(src, dst, send_sem, recv_sem, target):
        return pltpu.make_async_remote_copy(
            src_ref=src, dst_ref=dst, send_sem=send_sem, recv_sem=recv_sem,
            device_id=target, device_id_type=pl.DeviceIdType.MESH,
        )

    def rows_copy(spot, piece, sems, target):
        rows = pl.ds(pl.multiple_of(piece * piece_rows, piece_rows), piece_rows)
        ref = held.at[spot, rows, :]
        return remote(ref, ref, sems.at[spot, piece], held_recv.at[spot, piece], {"blk": target})

    def rows_up(spot, piece):
        return rows_copy(spot, piece, up_send, me + 2)

    def rows_down(spot, piece):
        return rows_copy(spot, piece, down_send, me - 2)

    def sum_up(spot, piece):
        return remote(
            run_up.at[spot, piece], got_up.at[spot, piece],
            sum_up_send.at[spot, piece], sum_up_recv.at[spot, piece], {"blk": me + 2},
        )

    def sum_down(spot, piece):
        return remote(
            run_down.at[spot, piece], got_down.at[spot, piece],
            sum_down_send.at[spot, piece], sum_down_recv.at[spot, piece], {"blk": me - 2},
        )

    def pass_copy(piece):
        return remote(
            pass_out.at[piece], pass_in.at[piece],
            pass_send.at[piece], pass_recv.at[piece], {"blk": partner},
        )

    def pair_copy(which):
        return remote(
            pair.at[which], pair.at[which], pair_sem.at[0], pair_sem.at[1], {"blk": partner}
        )

    def swap(spot):
        return remote(
            own_part.at[spot], other_part.at[spot],
            swap_send.at[spot], swap_recv.at[spot], {"sub": 1 - side},
        )

    def neg_copy(step, spot):
        target = ((place + step) % line) * 2 + lane
        return remote(
            turned_all.at[spot], turned_all.at[spot],
            neg_send.at[step], neg_recv.at[spot], {"blk": target},
        )

    loads = [
        pltpu.make_async_copy(q_hbm, held.at[place], load_sem.at[0]),
        pltpu.make_async_copy(p_hbm, pair.at[lane], load_sem.at[1]),
    ]
    for load in loads:
        load.start()
    barrier = pltpu.get_barrier_semaphore()
    for step in range(1, line):
        pl.semaphore_signal(
            barrier, inc=1, device_id={"blk": ((place + step) % line) * 2 + lane},
            device_id_type=pl.DeviceIdType.MESH,
        )
    pl.semaphore_signal(
        barrier, inc=1, device_id={"blk": partner}, device_id_type=pl.DeviceIdType.MESH
    )
    pl.semaphore_signal(
        barrier, inc=1, device_id={"sub": 1 - side}, device_id_type=pl.DeviceIdType.MESH
    )
    turned_all[place] = turned_ref[...]
    for load in loads:
        load.wait()
    pl.semaphore_wait(barrier, line + 1)

    pair_copy(lane).start()

    @pl.loop(0, ROW_PIECES)
    def _(piece):
        @pl.when(place < last)
        def _():
            rows_up(place, piece).start()

        @pl.when(place > 0)
        def _():
            rows_down(place, piece).start()

    for step in range(1, line):
        neg_copy(step, place).start()

    down_index = lax.broadcasted_iota(jnp.int32, (row_count, row_count), 0)
    across_index = lax.broadcasted_iota(jnp.int32, (row_count, row_count), 1)

    def score(spot):
        own_part[spot] = lax.dot_general(
            pair[...].reshape(2 * row_count, width), held[spot], (((1,), (1,)), ((), ())),
            preferred_element_type=jnp.float32,
        )
        swap(spot).start()

    def product(spot):
        swap(spot).wait()
        query_block = spot * 2 + lane
        for which in range(2):
            passage_block = place * 2 + which
            gap = (passage_block - query_block + HALF + owners) % owners
            near = (jnp.zeros((row_count, row_count), jnp.int32) + gap) <= 2 * HALF
            passage = down_index + passage_block * row_count
            diagonal = (passage == across_index + query_block * row_count).astype(jnp.float32)
            counts = jnp.zeros((row_count, row_count), jnp.float32)
            for k in range(neg_count):
                counts += (turned_all[spot, k : k + 1, :] == passage).astype(jnp.float32)
            rows = slice(which * row_count, (which + 1) * row_count)
            weights = pair_weights(
                own_part[spot, rows] + other_part[spot, rows], counts, near, diagonal, factor
            )
            columns = pl.ds(pl.multiple_of(spot * row_count, row_count), row_count)
            col_w[which, :, columns] = weights.astype(jnp.bfloat16)
            row_w[:, rows] = weights.T.astype(jnp.bfloat16)

        for piece in range(PIECES):
            columns = slice(piece * piece_cols, (piece + 1) * piece_cols)
            part[spot, piece] = jnp.dot(
                row_w[...], pair[:, :, columns].reshape(2 * row_count, piece_cols),
                preferred_element_type=jnp.float32,
            )

    def passage_sum(which, piece):
        columns = pl.ds(pl.multiple_of(piece * piece_cols, piece_cols), piece_cols)
        return jnp.dot(
            col_w[which], held[:, :, columns].reshape(line * row_count, piece_cols),
            preferred_element_type=jnp.float32,
        )

    def send_passage_sums():
        @pl.loop(0, PIECES)
        def _(piece):
            pass_out[piece] = passage_sum(1 - lane, piece).astype(jnp.bfloat16)
            pass_copy(piece).start()

    for far in range(1, line):
        @pl.loop(0, ROW_PIECES)
        def _(piece):
            @pl.when(place >= far)
            def _():
                rows_up(place - far, piece).wait_recv()

                @pl.when(place < last)
                def _():
                    rows_up(place - far, piece).start()

            @pl.when(place + far < line)
            def _():
                rows_down(place + far, piece).wait_recv()

                @pl.when(place > 0)
                def _():
                    rows_down(place + far, piece).start()

        if far == 1:
            pair_copy(1 - lane).wait_recv()

        below = place - far
        above = place + far
        for spot, ready in ((below, place >= far), (above, place + far < line)):
            @pl.when(ready)
            def _():
                score(spot)

        for spot, ready in ((below, place >= far), (above, place + far < line)):
            @pl.when(ready)
            def _():
                neg_copy(1, spot).wait_recv()
                product(spot)

        inner = (place > 0) & (place < last)
        if far == line - 2:
            @pl.when(inner)
            def _():
                send_passage_sums()

        spot = last - far
        low = place * 2 < line

        @pl.loop(0, PIECES + LAG)
        def _(step):
            piece = step - jnp.where(low, 0, LAG)

            @pl.when((place < far) & (piece >= 0) & (piece < PIECES))
            def _():
                @pl.when(place == 0)
                def _():
                    run_up[far, piece] = part[far, piece].astype(jnp.bfloat16)

                @pl.when(place > 0)
                def _():
                    sum_up(far, piece).wait_recv()
                    run_up[far, piece] = (
                        part[far, piece] + got_up[far, piece].astype(jnp.float32)
                    ).astype(jnp.bfloat16)

                sum_up(far, piece).start()

            other = step - jnp.where(low, LAG, 0)

            @pl.when((place > spot) & (other >= 0) & (other < PIECES))
            def _():
                @pl.when(place == last)
                def _():
                    run_down[spot, other] = part[spot, other].astype(jnp.bfloat16)

                @pl.when(place < last)
                def _():
                    sum_down(spot, other).wait_recv()
                    run_down[spot, other] = (
                        part[spot, other] + got_down[spot, other].astype(jnp.float32)
                    ).astype(jnp.bfloat16)

                sum_down(spot, other).start()

        if far == 1:
            score(place)
            product(place)

        if far == line - 1:
            @pl.when(jnp.logical_not(inner))
            def _():
                send_passage_sums()

    @pl.loop(0, PIECES)
    def _(piece):
        columns = pl.ds(pl.multiple_of(piece * piece_cols, piece_cols), piece_cols)
        mine = passage_sum(lane, piece)
        pass_copy(piece).wait_recv()
        gp_ref[:, columns] = (
            factor * (mine + pass_in[piece].astype(jnp.float32))
        ).astype(jnp.bfloat16)

    @pl.loop(0, PIECES)
    def _(piece):
        columns = pl.ds(pl.multiple_of(piece * piece_cols, piece_cols), piece_cols)

        @pl.when(place > 0)
        def _():
            sum_up(place, piece).wait_recv()
            part[place, piece] += got_up[place, piece].astype(jnp.float32)

        @pl.when(place < last)
        def _():
            sum_down(place, piece).wait_recv()
            part[place, piece] += got_down[place, piece].astype(jnp.float32)

        gq_ref[:, columns] = (factor * part[place, piece]).astype(jnp.bfloat16)

    pair_copy(lane).wait_send()
    for step in range(1, line):
        neg_copy(step, place).wait_send()

    @pl.loop(0, ROW_PIECES)
    def _(piece):
        for spot in range(line):
            @pl.when((place >= spot) & (place < last))
            def _():
                rows_up(spot, piece).wait_send()

            @pl.when((place <= spot) & (place > 0))
            def _():
                rows_down(spot, piece).wait_send()

    @pl.loop(0, PIECES)
    def _(piece):
        pass_copy(piece).wait_send()
        for spot in range(line):
            @pl.when(place < spot)
            def _():
                sum_up(spot, piece).wait_send()

            @pl.when(place > spot)
            def _():
                sum_down(spot, piece).wait_send()


def dense_local(queries, passages, negatives):
    row_count, width = queries.shape
    neg_count = negatives.shape[1]
    owners = lax.axis_size("blk")
    line = owners // 2
    piece_cols = width // PIECES
    turned = negatives.T
    out = jax.ShapeDtypeStruct((row_count, width), jnp.bfloat16)
    vmem = pl.BlockSpec(memory_space=pltpu.VMEM)
    anywhere = pl.BlockSpec(memory_space=pl.ANY)
    dma = pltpu.SemaphoreType.DMA
    sums = pltpu.VMEM((line, PIECES, row_count, piece_cols), jnp.bfloat16)
    grid = dma((line, PIECES))
    row_grid = dma((line, ROW_PIECES))
    return pl.pallas_call(
        functools.partial(grid_kernel, owners, neg_count),
        out_shape=(out, out),
        in_specs=[anywhere, anywhere, vmem],
        out_specs=(vmem, vmem),
        scratch_shapes=[
            pltpu.VMEM((line, row_count, width), jnp.bfloat16),
            pltpu.VMEM((2, row_count, width), jnp.bfloat16),
            pltpu.VMEM((line, neg_count, row_count), jnp.int32),
            pltpu.VMEM((line, 2 * row_count, row_count), jnp.float32),
            pltpu.VMEM((line, 2 * row_count, row_count), jnp.float32),
            pltpu.VMEM((row_count, 2 * row_count), jnp.bfloat16),
            pltpu.VMEM((2, row_count, line * row_count), jnp.bfloat16),
            pltpu.VMEM((line, PIECES, row_count, piece_cols), jnp.float32),
            sums,
            sums,
            sums,
            sums,
            pltpu.VMEM((PIECES, row_count, piece_cols), jnp.bfloat16),
            pltpu.VMEM((PIECES, row_count, piece_cols), jnp.bfloat16),
            dma((2,)),
            dma((line,)),
            dma((line,)),
            dma((2,)),
            dma((line,)),
            dma((line,)),
            row_grid,
            row_grid,
            row_grid,
            grid,
            grid,
            grid,
            grid,
            dma((PIECES,)),
            dma((PIECES,)),
        ],
        compiler_params=pltpu.CompilerParams(
            collective_id=0, has_side_effects=True, vmem_limit_bytes=60 * 1024 * 1024
        ),
        cost_estimate=pl.CostEstimate(
            flops=12 * row_count * row_count * owners * width // 2,
            bytes_accessed=8 * row_count * width,
            transcendentals=row_count * row_count * owners,
        ),
    )(queries, passages, turned)


def solution(mesh):
    owners = mesh.shape["blk"]
    body = dense_local if owners == 8 else local
    return jax.shard_map(
        body,
        mesh=mesh,
        in_specs=(
            P(("groups", "blk"), "sub"),
            P(("groups", "blk"), "sub"),
            P(("groups", "blk"), None),
        ),
        out_specs=(P(("groups", "blk"), "sub"), P(("groups", "blk"), "sub")),
        check_vma=False,
    )
```

```python
import functools
import math

import jax
import jax.numpy as jnp
from jax import lax
from jax.experimental import pallas as pl
from jax.experimental.pallas import tpu as pltpu
from jax.sharding import PartitionSpec as P

D = 4096
HALF = 2


LOGIT_SLOPE = 2.0
LOGIT_SHIFT = -1.0
HARD_WEIGHT = 2.0


def shifted(value, axis, steps):
    count = lax.axis_size(axis)
    pairs = [(source, (source + steps) % count) for source in range(count)]
    return lax.ppermute(value, axis, pairs)


def tile_step(queries, passage_rows, carried, grad_rows, offset, factor):
    partial_value = jnp.einsum(
        "id,jd->ij", queries, passage_rows, preferred_element_type=jnp.float32
    )
    scores = lax.psum(partial_value, "sub")
    weights = jax.nn.sigmoid(factor * scores + LOGIT_SHIFT)
    if offset == 0:
        weights = weights - jnp.eye(weights.shape[0], dtype=jnp.float32)
    coeffs = weights.astype(jnp.bfloat16)
    grad_rows = grad_rows + jnp.dot(coeffs, passage_rows, preferred_element_type=jnp.float32)
    carried = carried + jnp.einsum("ij,id->jd", coeffs, queries, preferred_element_type=jnp.float32)
    return (carried, grad_rows)


def local(queries, passages, negatives):
    factor = LOGIT_SLOPE / math.sqrt(D)
    row_count, width = queries.shape
    zeros_tile = jnp.zeros((row_count, width), jnp.float32)
    grad_rows = zeros_tile
    upper_block = passages
    lower_block = shifted(passages, "blk", 1)
    upper_accum = zeros_tile
    lower_accum = zeros_tile
    for turn_index in range(HALF + 1):
        upper_accum, grad_rows = tile_step(
            queries, upper_block, upper_accum, grad_rows, turn_index, factor
        )
        if turn_index < HALF:
            lower_accum, grad_rows = tile_step(
                queries, lower_block, lower_accum, grad_rows, -(turn_index + 1), factor
            )
            upper_block = shifted(upper_block, "blk", -1)
            upper_accum = shifted(upper_accum, "blk", -1)
        if turn_index < HALF - 1:
            lower_block = shifted(lower_block, "blk", 1)
            lower_accum = shifted(lower_accum.astype(jnp.bfloat16), "blk", 1).astype(
                lower_accum.dtype
            )
    window_pass = shifted(upper_accum, "blk", HALF) + shifted(lower_accum, "blk", -HALF)
    owners = lax.axis_size("blk")
    neg_count = negatives.shape[1]
    capacity = 8 * row_count // owners
    slot_count = row_count * neg_count
    flat_neg = negatives.reshape(-1)
    owner_of = flat_neg // row_count
    local_row = flat_neg % row_count
    onehot_owner = (owner_of[:, None] == jnp.arange(owners, dtype=jnp.int32)[None, :]).astype(
        jnp.int32
    )
    position = jnp.sum((jnp.cumsum(onehot_owner, axis=0) - 1) * onehot_owner, axis=1)
    slot_index = owner_of * capacity + position
    requests = (
        jnp.full((owners * capacity,), -1, jnp.int32)
        .at[slot_index]
        .set(local_row)
        .reshape(owners, capacity)
    )
    incoming = lax.all_to_all(requests, "blk", split_axis=0, concat_axis=0, tiled=True)
    is_live = incoming >= 0
    picked = jnp.where(is_live, incoming, 0)
    rows_out = jnp.take(passages, picked.reshape(-1), axis=0).reshape(owners, capacity, width)
    fetched = lax.all_to_all(rows_out, "blk", split_axis=0, concat_axis=0, tiled=True)
    slot_rows = jnp.take(fetched.reshape(owners * capacity, width), slot_index, axis=0).reshape(
        row_count, neg_count, width
    )
    hard_partial = jnp.einsum("rkd,rd->rk", slot_rows, queries, preferred_element_type=jnp.float32)
    hard_scores = lax.psum(hard_partial, "sub")
    hard_coeffs = (HARD_WEIGHT * jax.nn.sigmoid(factor * hard_scores + LOGIT_SHIFT)).astype(
        jnp.bfloat16
    )
    grad_rows = grad_rows + jnp.einsum(
        "rk,rkd->rd", hard_coeffs, slot_rows, preferred_element_type=jnp.float32
    )
    source_slot = (
        jnp.zeros((owners * capacity,), jnp.int32)
        .at[slot_index]
        .set(jnp.arange(slot_count, dtype=jnp.int32))
    )
    query_buffer = jnp.take(queries, source_slot // neg_count, axis=0).reshape(
        owners, capacity, width
    )
    arrived_rows = lax.all_to_all(query_buffer, "blk", split_axis=0, concat_axis=0, tiled=True)
    owner_partial = jnp.einsum(
        "scd,scd->sc", arrived_rows, rows_out, preferred_element_type=jnp.float32
    )
    owner_scores = lax.psum(owner_partial, "sub")
    owner_coeffs = jnp.where(
        is_live, HARD_WEIGHT * jax.nn.sigmoid(factor * owner_scores + LOGIT_SHIFT), 0.0
    ).astype(jnp.bfloat16)
    member = (
        jnp.arange(row_count, dtype=jnp.int32)[:, None] == picked.reshape(1, -1)
    ) & is_live.reshape(1, -1)
    weighted = jnp.where(member, owner_coeffs.reshape(1, -1), jnp.zeros((), jnp.bfloat16))
    hard_pass = jnp.dot(
        weighted, arrived_rows.reshape(owners * capacity, width), preferred_element_type=jnp.float32
    )
    grad_queries = (factor * grad_rows).astype(jnp.bfloat16)
    grad_passages = (factor * (window_pass + hard_pass)).astype(jnp.bfloat16)
    return (grad_queries, grad_passages)


def pair_weights(scores, counts, near, diagonal, factor):
    gate = jax.nn.sigmoid(factor * scores + LOGIT_SHIFT)
    window = jnp.where(near, gate - diagonal, 0.0).astype(jnp.bfloat16).astype(jnp.float32)
    hard = (HARD_WEIGHT * gate).astype(jnp.bfloat16).astype(jnp.float32)
    return window + counts * hard


PIECES = 8
ROW_PIECES = 4
LAG = 3


def grid_kernel(
    owners, neg_count, q_hbm, p_hbm, turned_ref, gq_ref, gp_ref,
    held, pair, turned_all, own_part, other_part, row_w, col_w, part,
    run_up, run_down, got_up, got_down, pass_out, pass_in,
    load_sem, neg_send, neg_recv, pair_sem, swap_send, swap_recv,
    up_send, down_send, held_recv,
    sum_up_send, sum_up_recv, sum_down_send, sum_down_recv, pass_send, pass_recv,
):
    factor = LOGIT_SLOPE / math.sqrt(D)
    row_count, width = q_hbm.shape
    line = owners // 2
    piece_rows = row_count // ROW_PIECES
    piece_cols = width // PIECES
    last = line - 1
    me = lax.axis_index("blk")
    side = lax.axis_index("sub")
    place = me // 2
    lane = me % 2
    partner = place * 2 + 1 - lane

    def remote(src, dst, send_sem, recv_sem, target):
        return pltpu.make_async_remote_copy(
            src_ref=src, dst_ref=dst, send_sem=send_sem, recv_sem=recv_sem,
            device_id=target, device_id_type=pl.DeviceIdType.MESH,
        )

    def rows_copy(spot, piece, sems, target):
        rows = pl.ds(pl.multiple_of(piece * piece_rows, piece_rows), piece_rows)
        ref = held.at[spot, rows, :]
        return remote(ref, ref, sems.at[spot, piece], held_recv.at[spot, piece], {"blk": target})

    def rows_up(spot, piece):
        return rows_copy(spot, piece, up_send, me + 2)

    def rows_down(spot, piece):
        return rows_copy(spot, piece, down_send, me - 2)

    def sum_up(spot, piece):
        return remote(
            run_up.at[spot, piece], got_up.at[spot, piece],
            sum_up_send.at[spot, piece], sum_up_recv.at[spot, piece], {"blk": me + 2},
        )

    def sum_down(spot, piece):
        return remote(
            run_down.at[spot, piece], got_down.at[spot, piece],
            sum_down_send.at[spot, piece], sum_down_recv.at[spot, piece], {"blk": me - 2},
        )

    def pass_copy(piece):
        return remote(
            pass_out.at[piece], pass_in.at[piece],
            pass_send.at[piece], pass_recv.at[piece], {"blk": partner},
        )

    def pair_copy(which):
        return remote(
            pair.at[which], pair.at[which], pair_sem.at[0], pair_sem.at[1], {"blk": partner}
        )

    def swap(spot):
        return remote(
            own_part.at[spot], other_part.at[spot],
            swap_send.at[spot], swap_recv.at[spot], {"sub": 1 - side},
        )

    def neg_copy(step, spot):
        target = ((place + step) % line) * 2 + lane
        return remote(
            turned_all.at[spot], turned_all.at[spot],
            neg_send.at[step], neg_recv.at[spot], {"blk": target},
        )

    loads = [
        pltpu.make_async_copy(q_hbm, held.at[place], load_sem.at[0]),
        pltpu.make_async_copy(p_hbm, pair.at[lane], load_sem.at[1]),
    ]
    for load in loads:
        load.start()
    barrier = pltpu.get_barrier_semaphore()
    for step in range(1, line):
        pl.semaphore_signal(
            barrier, inc=1, device_id={"blk": ((place + step) % line) * 2 + lane},
            device_id_type=pl.DeviceIdType.MESH,
        )
    pl.semaphore_signal(
        barrier, inc=1, device_id={"blk": partner}, device_id_type=pl.DeviceIdType.MESH
    )
    pl.semaphore_signal(
        barrier, inc=1, device_id={"sub": 1 - side}, device_id_type=pl.DeviceIdType.MESH
    )
    turned_all[place] = turned_ref[...]
    for load in loads:
        load.wait()
    pl.semaphore_wait(barrier, line + 1)

    pair_copy(lane).start()

    @pl.loop(0, ROW_PIECES)
    def _(piece):
        @pl.when(place < last)
        def _():
            rows_up(place, piece).start()

        @pl.when(place > 0)
        def _():
            rows_down(place, piece).start()

    for step in range(1, line):
        neg_copy(step, place).start()

    down_index = lax.broadcasted_iota(jnp.int32, (row_count, row_count), 0)
    across_index = lax.broadcasted_iota(jnp.int32, (row_count, row_count), 1)

    def score(spot):
        own_part[spot] = lax.dot_general(
            pair[...].reshape(2 * row_count, width), held[spot], (((1,), (1,)), ((), ())),
            preferred_element_type=jnp.float32,
        )
        swap(spot).start()

    def product(spot):
        swap(spot).wait()
        query_block = spot * 2 + lane
        for which in range(2):
            passage_block = place * 2 + which
            gap = (passage_block - query_block + HALF + owners) % owners
            near = (jnp.zeros((row_count, row_count), jnp.int32) + gap) <= 2 * HALF
            passage = down_index + passage_block * row_count
            diagonal = (passage == across_index + query_block * row_count).astype(jnp.float32)
            counts = jnp.zeros((row_count, row_count), jnp.float32)
            for k in range(neg_count):
                counts += (turned_all[spot, k : k + 1, :] == passage).astype(jnp.float32)
            rows = slice(which * row_count, (which + 1) * row_count)
            weights = pair_weights(
                own_part[spot, rows] + other_part[spot, rows], counts, near, diagonal, factor
            )
            columns = pl.ds(pl.multiple_of(spot * row_count, row_count), row_count)
            col_w[which, :, columns] = weights.astype(jnp.bfloat16)
            row_w[:, rows] = weights.T.astype(jnp.bfloat16)

        for piece in range(PIECES):
            columns = slice(piece * piece_cols, (piece + 1) * piece_cols)
            tile = jnp.dot(
                row_w[...], pair[:, :, columns].reshape(2 * row_count, piece_cols),
                preferred_element_type=jnp.float32,
            )
            part[spot, piece] = tile

            @pl.when((place == 0) & (spot > 0))
            def _():
                run_up[spot, piece] = tile.astype(jnp.bfloat16)
                sum_up(spot, piece).start()

            @pl.when((place == last) & (spot < last))
            def _():
                run_down[spot, piece] = tile.astype(jnp.bfloat16)
                sum_down(spot, piece).start()

    def passage_sum(which, piece):
        columns = pl.ds(pl.multiple_of(piece * piece_cols, piece_cols), piece_cols)
        return jnp.dot(
            col_w[which], held[:, :, columns].reshape(line * row_count, piece_cols),
            preferred_element_type=jnp.float32,
        )

    def send_passage_sums():
        @pl.loop(0, PIECES)
        def _(piece):
            pass_out[piece] = passage_sum(1 - lane, piece).astype(jnp.bfloat16)
            pass_copy(piece).start()

    for far in range(1, line):
        @pl.loop(0, ROW_PIECES)
        def _(piece):
            @pl.when(place >= far)
            def _():
                rows_up(place - far, piece).wait_recv()

                @pl.when(place < last)
                def _():
                    rows_up(place - far, piece).start()

            @pl.when(place + far < line)
            def _():
                rows_down(place + far, piece).wait_recv()

                @pl.when(place > 0)
                def _():
                    rows_down(place + far, piece).start()

        if far == 1:
            pair_copy(1 - lane).wait_recv()

        below = place - far
        above = place + far
        for spot, ready in ((below, place >= far), (above, place + far < line)):
            @pl.when(ready)
            def _():
                score(spot)

        for spot, ready in ((below, place >= far), (above, place + far < line)):
            @pl.when(ready)
            def _():
                neg_copy(1, spot).wait_recv()
                product(spot)

        inner = (place > 0) & (place < last)
        if far == line - 2:
            @pl.when(inner)
            def _():
                send_passage_sums()

        spot = last - far
        low = place * 2 < line

        @pl.loop(0, PIECES + LAG)
        def _(step):
            piece = step - jnp.where(low, 0, LAG)

            @pl.when((place > 0) & (place < far) & (piece >= 0) & (piece < PIECES))
            def _():
                sum_up(far, piece).wait_recv()
                run_up[far, piece] = (
                    part[far, piece] + got_up[far, piece].astype(jnp.float32)
                ).astype(jnp.bfloat16)
                sum_up(far, piece).start()

            other = step - jnp.where(low, LAG, 0)

            @pl.when((place < last) & (place > spot) & (other >= 0) & (other < PIECES))
            def _():
                sum_down(spot, other).wait_recv()
                run_down[spot, other] = (
                    part[spot, other] + got_down[spot, other].astype(jnp.float32)
                ).astype(jnp.bfloat16)
                sum_down(spot, other).start()

        if far == 1:
            score(place)
            product(place)

        if far == line - 1:
            @pl.when(jnp.logical_not(inner))
            def _():
                send_passage_sums()

    @pl.loop(0, PIECES)
    def _(piece):
        columns = pl.ds(pl.multiple_of(piece * piece_cols, piece_cols), piece_cols)
        mine = passage_sum(lane, piece)
        pass_copy(piece).wait_recv()
        gp_ref[:, columns] = (
            factor * (mine + pass_in[piece].astype(jnp.float32))
        ).astype(jnp.bfloat16)

    @pl.loop(0, PIECES)
    def _(piece):
        columns = pl.ds(pl.multiple_of(piece * piece_cols, piece_cols), piece_cols)

        @pl.when(place > 0)
        def _():
            sum_up(place, piece).wait_recv()
            part[place, piece] += got_up[place, piece].astype(jnp.float32)

        @pl.when(place < last)
        def _():
            sum_down(place, piece).wait_recv()
            part[place, piece] += got_down[place, piece].astype(jnp.float32)

        gq_ref[:, columns] = (factor * part[place, piece]).astype(jnp.bfloat16)

    pair_copy(lane).wait_send()
    for step in range(1, line):
        neg_copy(step, place).wait_send()

    @pl.loop(0, ROW_PIECES)
    def _(piece):
        for spot in range(line):
            @pl.when((place >= spot) & (place < last))
            def _():
                rows_up(spot, piece).wait_send()

            @pl.when((place <= spot) & (place > 0))
            def _():
                rows_down(spot, piece).wait_send()

    @pl.loop(0, PIECES)
    def _(piece):
        pass_copy(piece).wait_send()
        for spot in range(line):
            @pl.when(place < spot)
            def _():
                sum_up(spot, piece).wait_send()

            @pl.when(place > spot)
            def _():
                sum_down(spot, piece).wait_send()


def dense_local(queries, passages, negatives):
    row_count, width = queries.shape
    neg_count = negatives.shape[1]
    owners = lax.axis_size("blk")
    line = owners // 2
    piece_cols = width // PIECES
    turned = negatives.T
    out = jax.ShapeDtypeStruct((row_count, width), jnp.bfloat16)
    vmem = pl.BlockSpec(memory_space=pltpu.VMEM)
    anywhere = pl.BlockSpec(memory_space=pl.ANY)
    dma = pltpu.SemaphoreType.DMA
    sums = pltpu.VMEM((line, PIECES, row_count, piece_cols), jnp.bfloat16)
    grid = dma((line, PIECES))
    row_grid = dma((line, ROW_PIECES))
    return pl.pallas_call(
        functools.partial(grid_kernel, owners, neg_count),
        out_shape=(out, out),
        in_specs=[anywhere, anywhere, vmem],
        out_specs=(vmem, vmem),
        scratch_shapes=[
            pltpu.VMEM((line, row_count, width), jnp.bfloat16),
            pltpu.VMEM((2, row_count, width), jnp.bfloat16),
            pltpu.VMEM((line, neg_count, row_count), jnp.int32),
            pltpu.VMEM((line, 2 * row_count, row_count), jnp.float32),
            pltpu.VMEM((line, 2 * row_count, row_count), jnp.float32),
            pltpu.VMEM((row_count, 2 * row_count), jnp.bfloat16),
            pltpu.VMEM((2, row_count, line * row_count), jnp.bfloat16),
            pltpu.VMEM((line, PIECES, row_count, piece_cols), jnp.float32),
            sums,
            sums,
            sums,
            sums,
            pltpu.VMEM((PIECES, row_count, piece_cols), jnp.bfloat16),
            pltpu.VMEM((PIECES, row_count, piece_cols), jnp.bfloat16),
            dma((2,)),
            dma((line,)),
            dma((line,)),
            dma((2,)),
            dma((line,)),
            dma((line,)),
            row_grid,
            row_grid,
            row_grid,
            grid,
            grid,
            grid,
            grid,
            dma((PIECES,)),
            dma((PIECES,)),
        ],
        compiler_params=pltpu.CompilerParams(
            collective_id=0, has_side_effects=True, vmem_limit_bytes=60 * 1024 * 1024
        ),
        cost_estimate=pl.CostEstimate(
            flops=12 * row_count * row_count * owners * width // 2,
            bytes_accessed=8 * row_count * width,
            transcendentals=row_count * row_count * owners,
        ),
    )(queries, passages, turned)


def solution(mesh):
    owners = mesh.shape["blk"]
    body = dense_local if owners == 8 else local
    return jax.shard_map(
        body,
        mesh=mesh,
        in_specs=(
            P(("groups", "blk"), "sub"),
            P(("groups", "blk"), "sub"),
            P(("groups", "blk"), None),
        ),
        out_specs=(P(("groups", "blk"), "sub"), P(("groups", "blk"), "sub")),
        check_vma=False,
    )
```
